256 devices in a mesh: band: 64 (over x, y_hi, z), grid: 4 (over y_lo, core).
Axes of the slice: x: 4, y: 4 (y_hi: 2, y_lo: 2; y = y_hi * 2 + y_lo), z: 8, core: 2. Of those that a mesh axis runs over, the one named last changes fastest.
Arguments:
- bands: float32 [128, 96, 96, 96], P('band', 'grid'), may hold values from -6 to 6
Outputs:
- exchange_out: float32 [128, 96, 96, 96], P('band', 'grid')
The draws below stay inside these ranges and needn't reach their ends.
All inputs are finite; a program needn't handle non-finite values.
Results may differ from the reference program's by a relative error of at most 0.0091.
Values may be sent and summed in bfloat16 or wider, within the bound.
No kernel may reach another device: no remote copies, remote signals or barrier semaphores. Data moves between devices by JAX's collectives and lax.ppermute only.
A program may use at most 128 MiB of HBM per device.

```python
import jax
import jax.numpy as jnp
import numpy as np
from jax import lax

NG = 96
BD = 2
ROUNDS = 3
BLOCKS = 64
NBANDS = 128


def shard_levels(stream_key, extent, split, least, largest):
    level, own = 1.0, jax.random.fold_in(stream_key, 6)
    for dim, parts in split:
        draws = jnp.exp(jax.random.uniform(jax.random.fold_in(own, dim), (parts,), jnp.float32, least / len(split), largest / len(split)))
        level = level * jnp.repeat(draws, extent[dim] // parts).reshape([-1 if axis == dim else 1 for axis in range(len(extent))])
    return level


def bell_draw(own_key, dims, width, reach, split=(), kind=jnp.bfloat16):
    array = width * jax.random.normal(own_key, dims, jnp.float32)
    if split:
        array = array * shard_levels(own_key, dims, split, -0.22, 0.18)
    return jnp.clip(array, -reach, reach).astype(kind)


def setup_inputs(seed: int = 0) -> dict:
    keys = jax.random.split(jax.random.key(seed), 2)
    return {
        "bands": bell_draw(keys[0], (NBANDS, NG, NG, NG), 1.0, 6.0, ((0, 64), (1, 4)), jnp.float32),
    }


kernel_scale = 16.0
screen_sq = 0.05


def dft_table(length):
    half = length // 2
    rows = np.arange(length)
    freq = np.where(rows <= half, rows, rows - half)
    phase = 2.0 * np.pi * np.outer(freq, rows) / length
    return np.where((rows <= half)[:, None], np.cos(phase), np.sin(phase))


def frequency_weights(rows, length):
    half = length // 2
    freq = jnp.where(rows <= half, rows, rows - half).astype(jnp.float32)
    weight = jnp.where((rows == 0) | (rows == half), 1.0, 2.0).astype(jnp.float32) / length
    return freq, weight


def multiplier(rows_x, rows_y, rows_z, length):
    freq_x, weight_x = frequency_weights(rows_x, length)
    freq_y, weight_y = frequency_weights(rows_y, length)
    freq_z, weight_z = frequency_weights(rows_z, length)
    square = freq_x[:, None, None] ** 2 + freq_y[None, :, None] ** 2 + freq_z[None, None, :] ** 2
    scale = weight_x[:, None, None] * weight_y[None, :, None] * weight_z[None, None, :]
    return kernel_scale * scale / (square + screen_sq)


def apply_table(form, cosines, data):
    return jnp.einsum(form, cosines.astype(jnp.float32), data.astype(jnp.float32), precision=lax.Precision.HIGHEST)


def potential_of(density, cosines, weights):
    section_one = apply_table("cz,pxyz->pxyc", cosines, density).astype(jnp.bfloat16)
    section_two = apply_table("cy,pxyz->pxcz", cosines, section_one).astype(jnp.bfloat16)
    section_three = (weights[None] * apply_table("cx,pxyz->pcyz", cosines, section_two)).astype(jnp.bfloat16)
    section_four = apply_table("cx,pcyz->pxyz", cosines, section_three).astype(jnp.bfloat16)
    section_five = apply_table("cy,pxcz->pxyz", cosines, section_four).astype(jnp.bfloat16)
    return apply_table("cz,pxyc->pxyz", cosines, section_five).astype(jnp.bfloat16)


def reference(bands):
    length = bands.shape[1]
    copies = bands.astype(jnp.bfloat16).reshape(BLOCKS, BD, length, length, length)
    cosines = jnp.asarray(dft_table(length), jnp.bfloat16)
    indices = jnp.arange(length, dtype=jnp.int32)
    weights = multiplier(indices, indices, indices, length)
    summed = jnp.zeros((BLOCKS, BD, length, length, length), jnp.float32)
    for round_index in range(1, ROUNDS + 1):
        partners = jnp.roll(copies, round_index, axis=0)

        def one_block(pair_blocks):
            mine, other = pair_blocks
            density = (mine[:, None].astype(jnp.float32) * other[None].astype(jnp.float32)).astype(jnp.bfloat16)
            density = density.reshape(BD * BD, length, length, length)
            field = potential_of(density, cosines, weights).reshape(BD, BD, length, length, length)
            own = jnp.einsum("ijxyz,jxyz->ixyz", field.astype(jnp.float32), other.astype(jnp.float32), precision=lax.Precision.HIGHEST)
            given = jnp.einsum("ijxyz,ixyz->jxyz", field.astype(jnp.float32), mine.astype(jnp.float32), precision=lax.Precision.HIGHEST)
            return own, given.astype(jnp.bfloat16)

        own, given = lax.map(one_block, (copies, partners))
        summed = summed + own + jnp.roll(given, -round_index, axis=0).astype(jnp.float32)
    return (-summed).reshape(bands.shape)
```

```python
import functools

import jax
import jax.numpy as jnp
import numpy as np
from jax import lax
from jax.experimental import pallas as pl
from jax.experimental.pallas import tpu as pltpu
from jax.sharding import PartitionSpec as P


NG = 96
PAIRS = 12
ROWS = 144
THIRD = 48
LANES = 128
SLAB = PAIRS * ROWS
KERNEL_SCALE = 16.0
SCREEN_SQ = 0.05
AXES = ("band", "grid")
BF = jnp.bfloat16
F32 = jnp.float32
UNROLL = 2


def dft_table(length):
    half = length // 2
    rows = np.arange(length)
    freq = np.where(rows <= half, rows, rows - half)
    phase = 2.0 * np.pi * np.outer(freq, rows) / length
    return np.where((rows <= half)[:, None], np.cos(phase), np.sin(phase))


def z_tables():
    table = dft_table(NG)
    forward = np.zeros((3, LANES, 2 * LANES))
    inverse = np.zeros((3, 2 * LANES, LANES))
    for g in range(3):
        part = table[:, 32 * g : 32 * g + 32]
        forward[g, :NG, :NG] = table.T
        forward[g, NG:, LANES : LANES + NG] = part.T
        inverse[g, :NG, :NG] = table
        inverse[g, LANES : LANES + NG, NG:] = part
    return jnp.asarray(forward, BF), jnp.asarray(inverse, BF)


def multiplier():
    index = np.arange(NG)
    freq = np.where(index <= NG // 2, index, index - NG // 2).astype(np.float32)
    weight = (np.where((index == 0) | (index == NG // 2), 1.0, 2.0) / NG).astype(np.float32)
    lane_freq = jnp.asarray(np.pad(freq, (0, LANES - NG)))
    lane_weight = jnp.asarray(np.pad(weight, (0, LANES - NG)))
    freq, weight = jnp.asarray(freq), jnp.asarray(weight)
    freq_b, weight_b = freq.reshape(48, 1, 2, 1), weight.reshape(48, 1, 2, 1)
    square = freq[None, :, None, None] ** 2 + freq_b**2 + lane_freq**2
    scale = weight[None, :, None, None] * weight_b * lane_weight
    return (KERNEL_SCALE * scale / (square + SCREEN_SQ)).reshape(48 * NG, 2 * LANES)


def dot(left, right):
    return jnp.dot(left, right, preferred_element_type=F32)


def pack_kernel(place, bands, *outs):
    high, core = place[0], place[1]
    mix = high ^ core
    for p in range(bands.shape[1] // 2):
        packed = []
        for band in range(2):
            first, second = bands[band, 2 * p], bands[band, 2 * p + 1]
            heads = (first[:THIRD], first[THIRD:], second[:THIRD])
            packed.append(
                jnp.concatenate(
                    [
                        jnp.concatenate([heads[g], second[THIRD:, 32 * g : 32 * g + 32]], axis=1)
                        for g in range(3)
                    ],
                    axis=0,
                )
            )
        for n, flag in enumerate((core, mix, high)):
            same, other = (
                jnp.where(flag == 0, packed[0], packed[1]),
                jnp.where(flag == 0, packed[1], packed[0]),
            )
            outs[2 * n][pl.ds(p * ROWS, ROWS)] = same.astype(BF)
            outs[2 * n + 1][pl.ds(p * ROWS, ROWS)] = other.astype(BF)


def pack(place, bands):
    steps = 3
    per = PAIRS // steps
    return pl.pallas_call(
        pack_kernel,
        grid=(steps,),
        in_specs=[
            pl.BlockSpec(memory_space=pltpu.SMEM),
            pl.BlockSpec((2, 2 * per, NG, NG), lambda i: (0, i, 0, 0)),
        ],
        out_specs=[pl.BlockSpec((per * ROWS, LANES), lambda i: (i, 0))] * 6,
        out_shape=[jax.ShapeDtypeStruct((SLAB, LANES), BF)] * 6,
        compiler_params=pltpu.CompilerParams(vmem_limit_bytes=48 << 20),
        name="pack",
    )(place, bands)


def unpack_kernel(place, *refs):
    a0, a1, a2, a3, b0, b1, b2, b3, c0, c2, out = refs
    high, core = place[0], place[1]
    mix = high ^ core
    for p in range(out.shape[1] // 2):
        rows = pl.ds(p * ROWS, ROWS)
        load = lambda ref: ref[rows].astype(F32)
        terms = (
            (core, load(a0) + load(a2), load(a1) + load(a3)),
            (mix, load(b0) + load(b3), load(b1) + load(b2)),
            (high, load(c0), load(c2)),
        )
        for band in range(2):
            total = sum(jnp.where(flag == band, same, other) for flag, same, other in terms)
            total = -total
            out[band, 2 * p] = total[: 2 * THIRD, :NG]
            tail = [total[THIRD * g : THIRD * g + THIRD, NG:] for g in range(3)]
            out[band, 2 * p + 1, :THIRD] = total[2 * THIRD :, :NG]
            out[band, 2 * p + 1, THIRD:] = jnp.concatenate(tail, axis=1)


def unpack(place, parts):
    steps = 3
    per = PAIRS // steps
    return pl.pallas_call(
        unpack_kernel,
        grid=(steps,),
        in_specs=[pl.BlockSpec(memory_space=pltpu.SMEM)]
        + [pl.BlockSpec((per * ROWS, LANES), lambda i: (i, 0))] * 10,
        out_specs=pl.BlockSpec((2, 2 * per, NG, NG), lambda i: (0, i, 0, 0)),
        out_shape=jax.ShapeDtypeStruct((2, 2 * PAIRS, NG, NG), F32),
        compiler_params=pltpu.CompilerParams(vmem_limit_bytes=48 << 20),
        name="unpack",
    )(place, *parts)


def transform(left, right, tables, grid_values, emit):
    y_table, y_back, x_table, x_back, z_table, z_back, weights = tables

    for r in range(4):

        def forward(p, carry, r=r):
            rows = pl.ds(pl.multiple_of(p * ROWS, ROWS), ROWS)
            density = left[r][rows] * right[r][rows]
            parts = [dot(density[THIRD * g : THIRD * g + THIRD], z_table[g]) for g in range(3)]
            one = jnp.concatenate([parts[0][:, :LANES], parts[1][:, :LANES]], axis=0)
            tail = parts[0][:, LANES:] + parts[1][:, LANES:] + parts[2][:, LANES:]
            two = jnp.concatenate([parts[2][:, :LANES], tail], axis=0)
            lines = dot(y_table[...], jnp.concatenate([one, two], axis=1).astype(BF))
            x = r * 2 * PAIRS + 2 * p
            grid_values[pl.ds(x, NG, stride=NG), :] = lines[:, :LANES]
            grid_values[pl.ds(x + 1, NG, stride=NG), :] = lines[:, LANES:]
            return carry

        lax.fori_loop(0, PAIRS, forward, 0, unroll=UNROLL)

    def middle(q, carry):
        upper = pl.ds(pl.multiple_of(q * 2 * NG, 2 * NG), NG)
        lower = pl.ds(pl.multiple_of(q * 2 * NG + NG, NG), NG)
        block = jnp.concatenate([grid_values[upper, :], grid_values[lower, :]], axis=1).astype(BF)
        scaled = weights[pl.ds(pl.multiple_of(q * NG, NG), NG), :] * dot(x_table[...], block)
        back = dot(x_back[...], scaled.astype(BF))
        grid_values[upper, :] = back[:, :LANES]
        grid_values[lower, :] = back[:, LANES:]
        return carry

    lax.fori_loop(0, NG // 2, middle, 0, unroll=2 * UNROLL)

    for r in range(4):

        def inverse(p, carry, r=r):
            x = r * 2 * PAIRS + 2 * p
            one = grid_values[pl.ds(x, NG, stride=NG), :]
            two = grid_values[pl.ds(x + 1, NG, stride=NG), :]
            lines = dot(y_back[...], jnp.concatenate([one, two], axis=1).astype(BF)).astype(BF)
            one, two = lines[:, :LANES], lines[:, LANES:]
            heads = (one[:THIRD], one[THIRD:], two[:THIRD])
            potential = jnp.concatenate(
                [
                    dot(jnp.concatenate([heads[g], two[THIRD:]], axis=1), z_back[g])
                    for g in range(3)
                ],
                axis=0,
            ).astype(BF)
            emit(r, pl.ds(pl.multiple_of(p * ROWS, ROWS), ROWS), potential)
            return carry

        lax.fori_loop(0, PAIRS, inverse, 0, unroll=UNROLL)


def first_kernel(*refs):
    tables, refs = refs[:7], refs[7:]
    a, b, field_ab, grid_values = refs[:4], refs[4:8], refs[8:12], refs[12]

    def emit(r, rows, potential):
        field_ab[r][rows] = potential

    transform(a, b, tables, grid_values, emit)


def second_kernel(*refs):
    tables, refs = refs[:7], refs[7:]
    a, b, c, field_ab = refs[:4], refs[4:8], refs[8:12], refs[12:16]
    field_ac, out_a, grid_values = refs[16:20], refs[20:24], refs[24]

    def emit(r, rows, potential):
        field_ac[r][rows] = potential
        total = field_ab[r][rows].astype(F32) * b[r][rows].astype(F32)
        total += potential.astype(F32) * c[r][rows].astype(F32)
        out_a[r][rows] = total.astype(BF)

    transform(a, c, tables, grid_values, emit)


def third_kernel(*refs):
    tables, refs = refs[:7], refs[7:]
    a, b, c, field_ab, field_ac = (refs[4 * n : 4 * n + 4] for n in range(5))
    out_b, out_keep, out_give, grid_values = refs[20:24], refs[24], refs[25], refs[26]

    def emit(r, rows, potential):
        field = potential.astype(F32)
        one, two, three = (v[r][rows].astype(F32) for v in (a, b, c))
        out_b[r][rows] = (field_ab[r][rows].astype(F32) * one + field * three).astype(BF)
        total = (field_ac[r][rows].astype(F32) * one + field * two).astype(BF)
        target = (out_keep, out_give)[r % 2]
        target[pl.ds(pl.multiple_of(rows.start + (r // 2) * SLAB, ROWS), ROWS)] = total

    transform(b, c, tables, grid_values, emit)


def call_transform(kernel, name, tables, slabs, out_slabs):
    flops = 2 * 6 * NG**4
    return pl.pallas_call(
        kernel,
        in_specs=[pl.BlockSpec(memory_space=pltpu.VMEM)] * (7 + len(slabs)),
        out_specs=[pl.BlockSpec(memory_space=pltpu.VMEM)] * len(out_slabs),
        out_shape=[jax.ShapeDtypeStruct((n * SLAB, LANES), BF) for n in out_slabs],
        scratch_shapes=[pltpu.VMEM((NG * NG, LANES), F32)],
        compiler_params=pltpu.CompilerParams(vmem_limit_bytes=50 << 20),
        cost_estimate=pl.CostEstimate(flops=flops * 10, bytes_accessed=12 << 20, transcendentals=0),
        name=name,
    )(*tables, *slabs)


def sum_kernel(kept, received, *outs):
    total = (kept[...].astype(F32) + received[...].astype(F32)).astype(BF)
    outs[0][...] = total[:SLAB]
    outs[1][...] = total[SLAB:]


def add_halves(kept, received):
    return pl.pallas_call(
        sum_kernel,
        in_specs=[pl.BlockSpec(memory_space=pltpu.VMEM)] * 2,
        out_specs=[pl.BlockSpec(memory_space=pltpu.VMEM)] * 2,
        out_shape=[jax.ShapeDtypeStruct((SLAB, LANES), BF)] * 2,
        name="add_halves",
    )(kept, received)


def passed(value, blocks, by, length):
    pairs = [
        (4 * k + s, 4 * ((k + by) % length) + (s ^ blocks)) for k in range(length) for s in range(4)
    ]
    return lax.ppermute(value, AXES, pairs)


def per_device(bands):
    length = lax.axis_size("band")
    me = lax.axis_index("grid")
    place = jnp.stack([me // 2, me % 2]).astype(jnp.int32)
    send = functools.partial(passed, length=length)

    core_same, core_other, mix_same, mix_other, high_same, high_other = pack(place, bands)
    c = [send(high_same, 0, 2), None, send(high_other, 2, 2), None]
    b = [mix_same, send(mix_other, 1, 0), send(mix_other, 2, 0), send(mix_same, 3, 0)]
    a = [send((core_same, core_other)[r % 2], r, -1) for r in range(4)]
    c[1], c[3] = send(c[0], 1, 0), send(c[2], 1, 0)

    table = dft_table(NG)
    orders = [np.concatenate([np.arange(24) + 24 * (r ^ s) for r in range(4)]) for s in range(4)]
    x_tables = jnp.asarray(np.stack([table[:, order] for order in orders]), BF)
    x_table = lax.dynamic_index_in_dim(x_tables, me, 0, keepdims=False)
    x_backs = jnp.asarray(np.stack([table[:, order].T for order in orders]), BF)
    x_back = lax.dynamic_index_in_dim(x_backs, me, 0, keepdims=False)
    y_table, y_back = jnp.asarray(table, BF), jnp.asarray(table.T, BF)
    z_table, z_back = z_tables()
    tables = (y_table, y_back, x_table, x_back, z_table, z_back, multiplier())

    field_ab = call_transform(first_kernel, "pair_ab", tables, [*a, *b], [1] * 4)
    outs = call_transform(second_kernel, "pair_ac", tables, [*a, *b, *c, *field_ab], [1] * 8)
    field_ac, out_a = outs[:4], outs[4:]
    back_a = [send(out_a[r], r, 1) for r in range(4)]
    outs = call_transform(
        third_kernel, "pair_bc", tables, [*a, *b, *c, *field_ab, *field_ac], [1] * 4 + [2] * 2
    )
    out_b, kept, given = outs[:4], outs[4], outs[5]
    c0, c2 = add_halves(kept, send(given, 1, 0))
    back_c = [send(c0, 0, -2), send(c2, 2, -2)]
    back_b = [out_b[0]] + [send(out_b[r], r, 0) for r in range(1, 4)]
    return unpack(place, [*back_a, *back_b, *back_c])


def solution(mesh):
    spec = P("band", "grid", None, None)
    return jax.shard_map(
        per_device, mesh=mesh, in_specs=(spec,), out_specs=spec, check_vma=False
    )
```

```python
import functools

import jax
import jax.numpy as jnp
import numpy as np
from jax import lax
from jax.experimental import pallas as pl
from jax.experimental.pallas import tpu as pltpu
from jax.sharding import PartitionSpec as P


NG = 96
PAIRS = 12
ROWS = 144
THIRD = 48
LANES = 128
SLAB = PAIRS * ROWS
KERNEL_SCALE = 16.0
SCREEN_SQ = 0.05
AXES = ("band", "grid")
BF = jnp.bfloat16
F32 = jnp.float32
BATCH = 6
SMALL_VMEM = 24 << 20
LARGE_VMEM = 30 << 20


def dft_table(length):
    half = length // 2
    rows = np.arange(length)
    freq = np.where(rows <= half, rows, rows - half)
    phase = 2.0 * np.pi * np.outer(freq, rows) / length
    return np.where((rows <= half)[:, None], np.cos(phase), np.sin(phase))


def z_tables():
    table = dft_table(NG)
    forward = np.zeros((3, LANES, 2 * LANES))
    inverse = np.zeros((3, 2 * LANES, LANES))
    for g in range(3):
        part = table[:, 32 * g : 32 * g + 32]
        forward[g, :NG, :NG] = table.T
        forward[g, NG:, LANES : LANES + NG] = part.T
        inverse[g, :NG, :NG] = table
        inverse[g, LANES : LANES + NG, NG:] = part
    return jnp.asarray(forward, BF), jnp.asarray(inverse, BF)


def multiplier_parts():
    index = np.arange(NG)
    freq = np.where(index <= NG // 2, index, index - NG // 2).astype(np.float32)
    weight = (np.where((index == 0) | (index == NG // 2), 1.0, 2.0) / NG).astype(np.float32)
    pad = lambda v: np.pad(v, (0, LANES - NG))
    square = (freq**2).reshape(NG // 2, 2, 1) + pad(freq**2)
    scale = np.float32(KERNEL_SCALE) * weight.reshape(NG // 2, 2, 1) * pad(weight)
    wide = lambda v: np.broadcast_to(v[:, None], (NG, 2 * LANES))
    tall = lambda v: v.reshape(NG // 2, 2 * LANES)
    return [jnp.asarray(v, F32) for v in (wide(freq**2), wide(weight), tall(square), tall(scale))]


def multiplier_kernel(freq, weight, square, scale, out):
    for q in range(NG // 2):
        total = freq[...] + square[q : q + 1, :] + SCREEN_SQ
        out[q * NG : q * NG + NG, :] = weight[...] * scale[q : q + 1, :] / total


def multiplier():
    return pl.pallas_call(
        multiplier_kernel,
        out_shape=jax.ShapeDtypeStruct((NG // 2 * NG, 2 * LANES), F32),
        compiler_params=pltpu.CompilerParams(vmem_limit_bytes=SMALL_VMEM),
        name="multiplier",
    )(*multiplier_parts())


def dot(left, right):
    return jnp.dot(left, right, preferred_element_type=F32)


def pack_kernel(place, bands, for_a, for_b, b_keep, b_give, c_same, c_other):
    high, core = place[0], place[1]
    mix = high ^ core
    for p in range(bands.shape[1] // 2):
        packed = []
        for band in range(2):
            first, second = bands[band, 2 * p], bands[band, 2 * p + 1]
            heads = (first[:THIRD], first[THIRD:], second[:THIRD])
            rows = [
                jnp.concatenate([heads[g], second[THIRD:, 32 * g : 32 * g + 32]], axis=1)
                for g in range(3)
            ]
            packed.append(jnp.concatenate(rows, axis=0))
        pick = lambda flag: jnp.where(flag == 0, packed[0], packed[1]).astype(BF)
        for_a[0, p], for_a[1, p] = pick(core), pick(1 - core)
        mix_same, mix_other = pick(mix), pick(1 - mix)
        for_b[0, p], for_b[1, p] = mix_other, mix_same
        b_keep[p], b_give[p] = mix_same, mix_other
        c_same[p], c_other[p] = pick(high), pick(1 - high)


def one_slab(per):
    return pl.BlockSpec((per, ROWS, LANES), lambda i: (i, 0, 0))


def two_slabs(per):
    return pl.BlockSpec((2, per, ROWS, LANES), lambda i: (0, i, 0, 0))


def shape_of(count):
    dims = (PAIRS, ROWS, LANES)
    return jax.ShapeDtypeStruct(dims if count == 1 else (count, *dims), BF)


def pack(place, bands):
    steps = 3
    per = PAIRS // steps
    return pl.pallas_call(
        pack_kernel,
        grid=(steps,),
        in_specs=[
            pl.BlockSpec(memory_space=pltpu.SMEM),
            pl.BlockSpec((2, 2 * per, NG, NG), lambda i: (0, i, 0, 0)),
        ],
        out_specs=[two_slabs(per)] * 2 + [one_slab(per)] * 4,
        out_shape=[shape_of(2)] * 2 + [shape_of(1)] * 4,
        compiler_params=pltpu.CompilerParams(vmem_limit_bytes=SMALL_VMEM),
        name="pack",
    )(place, bands)


def unpack_kernel(place, a_same, a_cross, b_cross, b_own, b_mate, c_same, c_cross, out):
    high, core = place[0], place[1]
    mix = high ^ core
    for p in range(out.shape[1] // 2):
        load = lambda ref, *at: ref[(*at, p)].astype(F32)
        terms = (
            (core, load(a_same, 0) + load(a_cross, 0), load(a_same, 1) + load(a_cross, 1)),
            (mix, load(b_own) + load(b_cross, 1), load(b_mate, 0) + load(b_cross, 0)),
            (high, load(c_same), load(c_cross)),
        )
        for band in range(2):
            total = -sum(jnp.where(flag == band, same, other) for flag, same, other in terms)
            out[band, 2 * p] = total[: 2 * THIRD, :NG]
            tail = [total[THIRD * g : THIRD * g + THIRD, NG:] for g in range(3)]
            out[band, 2 * p + 1, :THIRD] = total[2 * THIRD :, :NG]
            out[band, 2 * p + 1, THIRD:] = jnp.concatenate(tail, axis=1)


def unpack(place, *parts):
    steps = 3
    per = PAIRS // steps
    specs = {3: one_slab(per), 4: two_slabs(per)}
    return pl.pallas_call(
        unpack_kernel,
        grid=(steps,),
        in_specs=[pl.BlockSpec(memory_space=pltpu.SMEM)] + [specs[v.ndim] for v in parts],
        out_specs=pl.BlockSpec((2, 2 * per, NG, NG), lambda i: (0, i, 0, 0)),
        out_shape=jax.ShapeDtypeStruct((2, 2 * PAIRS, NG, NG), F32),
        compiler_params=pltpu.CompilerParams(vmem_limit_bytes=SMALL_VMEM),
        name="unpack",
    )(place, *parts)


def transform(left, right, tables, grid_values, lines, emit):
    y_table, y_back, x_table, x_back, z_table, z_back, weights = tables
    flat = lambda v: v.reshape(-1, v.shape[-1])

    for r in range(4):
        held = lines.at[r % 2]

        def forward_z(i, carry, r=r, held=held):
            part = pl.ds(i * BATCH, BATCH)
            density = left[r][part] * right[r][part]
            sums = [
                dot(flat(density[:, THIRD * g : THIRD * g + THIRD]), z_table[g]) for g in range(3)
            ]
            tail = sums[0][:, LANES:] + sums[1][:, LANES:] + sums[2][:, LANES:]
            keep = lambda v: v.astype(BF).reshape(BATCH, THIRD, LANES)
            held[part, :THIRD, :LANES] = keep(sums[0][:, :LANES])
            held[part, THIRD:, :LANES] = keep(sums[1][:, :LANES])
            held[part, :THIRD, LANES:] = keep(sums[2][:, :LANES])
            held[part, THIRD:, LANES:] = keep(tail)
            return carry

        def forward_y(p, carry, r=r, held=held):
            values = dot(y_table[...], held[p])
            x = r * 2 * PAIRS + 2 * p
            grid_values[pl.ds(x, NG, stride=NG), :] = values[:, :LANES]
            grid_values[pl.ds(x + 1, NG, stride=NG), :] = values[:, LANES:]
            return carry

        lax.fori_loop(0, PAIRS // BATCH, forward_z, 0, unroll=True)
        lax.fori_loop(0, PAIRS, forward_y, 0, unroll=True)

    def middle(q, carry):
        upper = pl.ds(pl.multiple_of(q * 2 * NG, 2 * NG), NG)
        lower = pl.ds(pl.multiple_of(q * 2 * NG + NG, NG), NG)
        block = jnp.concatenate([grid_values[upper, :], grid_values[lower, :]], axis=1).astype(BF)
        scaled = weights[pl.ds(pl.multiple_of(q * NG, NG), NG), :] * dot(x_table[...], block)
        back = dot(x_back[...], scaled.astype(BF))
        grid_values[upper, :] = back[:, :LANES]
        grid_values[lower, :] = back[:, LANES:]
        return carry

    lax.fori_loop(0, NG // 2, middle, 0, unroll=16)

    for r in range(4):
        held = lines.at[r % 2]

        def inverse_y(p, carry, r=r, held=held):
            x = r * 2 * PAIRS + 2 * p
            one = grid_values[pl.ds(x, NG, stride=NG), :]
            two = grid_values[pl.ds(x + 1, NG, stride=NG), :]
            held[p] = dot(y_back[...], jnp.concatenate([one, two], axis=1).astype(BF)).astype(BF)
            return carry

        def inverse_z(i, carry, r=r, held=held):
            part = pl.ds(i * BATCH, BATCH)
            last = flat(held[part, THIRD:, LANES:])
            heads = (
                held[part, :THIRD, :LANES],
                held[part, THIRD:, :LANES],
                held[part, :THIRD, LANES:],
            )
            for g in range(3):
                values = dot(jnp.concatenate([flat(heads[g]), last], axis=1), z_back[g])
                at = (part, slice(THIRD * g, THIRD * g + THIRD))
                emit(r, at, values.astype(BF).reshape(BATCH, THIRD, LANES))
            return carry

        lax.fori_loop(0, PAIRS, inverse_y, 0, unroll=True)
        lax.fori_loop(0, PAIRS // BATCH, inverse_z, 0, unroll=True)


def whole(first, second, odd):
    part = lambda ref: ref if len(ref.shape) == 3 else ref.at[0]
    return [part(first), odd.at[0], part(second), odd.at[1]]


def first_kernel(*refs):
    a, b, refs = whole(*refs[7:10]), whole(*refs[10:13]), (*refs[:7], *refs[13:])
    field_ab, scratch = refs[7], refs[8:]

    def emit(r, at, potential):
        field_ab[(r, *at)] = potential

    transform(a, b, refs[:7], *scratch, emit)


def second_kernel(*refs):
    a, b, c = (whole(*refs[7 + 3 * n : 10 + 3 * n]) for n in range(3))
    field_ab, field_ac, out_own, out_cross, out_give = refs[16:21]
    out = (out_own, out_give.at[0], out_cross, out_give.at[1])

    def emit(r, at, potential):
        field_ac[(r, *at)] = potential
        total = field_ab[(r, *at)].astype(F32) * b[r][at].astype(F32)
        out[r][at] = (total + potential.astype(F32) * c[r][at].astype(F32)).astype(BF)

    transform(a, c, refs[:7], *refs[21:], emit)


def third_kernel(*refs):
    a, b, c = (whole(*refs[7 + 3 * n : 10 + 3 * n]) for n in range(3))
    field_ab, field_ac, b_own, b_cross, b_give, c_keep, c_give = refs[16:23]
    out_b = (b_own, b_give.at[0], b_cross, b_give.at[1])
    out_c = (c_keep.at[0], c_give.at[0], c_keep.at[1], c_give.at[1])

    def emit(r, at, potential):
        field = potential.astype(F32)
        one, two, three = (v[r][at].astype(F32) for v in (a, b, c))
        out_b[r][at] = (field_ab[(r, *at)].astype(F32) * one + field * three).astype(BF)
        out_c[r][at] = (field_ac[(r, *at)].astype(F32) * one + field * two).astype(BF)

    transform(b, c, refs[:7], *refs[23:], emit)


def call_transform(kernel, name, tables, slabs, outs):
    return pl.pallas_call(
        kernel,
        in_specs=[pl.BlockSpec(memory_space=pltpu.VMEM)] * (len(tables) + len(slabs)),
        out_specs=[pl.BlockSpec(memory_space=pltpu.VMEM)] * len(outs),
        out_shape=[shape_of(count) for count in outs],
        scratch_shapes=[
            pltpu.VMEM((NG * NG, LANES), F32),
            pltpu.VMEM((2, PAIRS, NG, 2 * LANES), BF),
        ],
        compiler_params=pltpu.CompilerParams(vmem_limit_bytes=LARGE_VMEM),
        cost_estimate=pl.CostEstimate(
            flops=10 * 12 * NG**4, bytes_accessed=12 << 20, transcendentals=0
        ),
        name=name,
    )(*tables, *slabs)


def sum_kernel(kept, received, same, cross):
    for n, out in enumerate((same, cross)):
        out[...] = (kept[n].astype(F32) + received[n].astype(F32)).astype(BF)


def add_halves(kept, received):
    return pl.pallas_call(
        sum_kernel,
        out_shape=[shape_of(1)] * 2,
        compiler_params=pltpu.CompilerParams(vmem_limit_bytes=SMALL_VMEM),
        name="add_halves",
    )(kept, received)


def passed(value, blocks, by, length):
    pairs = [
        (4 * k + s, 4 * ((k + by) % length) + (s ^ blocks)) for k in range(length) for s in range(4)
    ]
    return lax.ppermute(value, AXES, pairs)


def per_device(bands):
    length = lax.axis_size("band")
    me = lax.axis_index("grid")
    place = jnp.stack([me // 2, me % 2]).astype(jnp.int32)
    send = functools.partial(passed, length=length)

    for_a, for_b, b_keep, b_give, c_same, c_other = pack(place, bands)
    c_same, c_cross = send(c_same, 0, 2), send(c_other, 2, 2)
    b_cross = send(for_b, 2, 0)
    a_same, a_cross = send(for_a, 0, -1), send(for_a, 2, -1)
    b = [b_keep, b_cross, send(jnp.stack([b_give, b_cross[1]]), 1, 0)]
    a = [a_same, a_cross, send(jnp.stack([a_same[1], a_cross[1]]), 1, 0)]
    c = [c_same, c_cross, send(jnp.stack([c_same, c_cross]), 1, 0)]

    table = dft_table(NG)
    orders = [np.concatenate([np.arange(24) + 24 * (r ^ s) for r in range(4)]) for s in range(4)]
    both = np.stack([np.stack([table[:, order], table[:, order].T]) for order in orders])
    x_table, x_back = lax.dynamic_index_in_dim(jnp.asarray(both, BF), me, 0, keepdims=False)
    y_table, y_back = jnp.asarray(table, BF), jnp.asarray(table.T, BF)
    tables = (y_table, y_back, x_table, x_back, *z_tables(), multiplier())

    (field_ab,) = call_transform(first_kernel, "pair_ab", tables, [*a, *b], [4])
    field_ac, a_own, a_far, a_give = call_transform(
        second_kernel, "pair_ac", tables, [*a, *b, *c, field_ab], [4, 1, 1, 2]
    )
    a_mate = send(a_give, 1, 0)
    a_same = send(jnp.stack([a_own, a_mate[0]]), 0, 1)
    a_cross = send(jnp.stack([a_far, a_mate[1]]), 2, 1)
    b_own, b_far, b_give, c_keep, c_give = call_transform(
        third_kernel, "pair_bc", tables, [*a, *b, *c, field_ab, field_ac], [1, 1, 2, 2, 2]
    )
    c_same, c_cross = add_halves(c_keep, send(c_give, 1, 0))
    c_same, c_cross = send(c_same, 0, -2), send(c_cross, 2, -2)
    b_mate = send(b_give, 1, 0)
    b_cross = send(jnp.stack([b_far, b_mate[1]]), 2, 0)
    return unpack(place, a_same, a_cross, b_cross, b_own, b_mate, c_same, c_cross)


def solution(mesh):
    spec = P("band", "grid", None, None)
    return jax.shard_map(
        per_device, mesh=mesh, in_specs=(spec,), out_specs=spec, check_vma=False
    )
```

```python
import functools

import jax
import jax.numpy as jnp
import numpy as np
from jax import lax
from jax.experimental import pallas as pl
from jax.experimental.pallas import tpu as pltpu
from jax.sharding import PartitionSpec as P


NG = 96
PAIRS = 12
ROWS = 144
THIRD = 48
LANES = 128
SLAB = PAIRS * ROWS
KERNEL_SCALE = 16.0
SCREEN_SQ = 0.05
AXES = ("band", "grid")
BF = jnp.bfloat16
F32 = jnp.float32
BATCH = 6
SMALL_VMEM = 24 << 20
LARGE_VMEM = 30 << 20


def dft_table(length):
    half = length // 2
    rows = np.arange(length)
    freq = np.where(rows <= half, rows, rows - half)
    phase = 2.0 * np.pi * np.outer(freq, rows) / length
    return np.where((rows <= half)[:, None], np.cos(phase), np.sin(phase))


def z_tables():
    table = dft_table(NG)
    forward = np.zeros((3, LANES, 2 * LANES))
    inverse = np.zeros((3, 2 * LANES, LANES))
    for g in range(3):
        part = table[:, 32 * g : 32 * g + 32]
        forward[g, :NG, :NG] = table.T
        forward[g, NG:, LANES : LANES + NG] = part.T
        inverse[g, :NG, :NG] = table
        inverse[g, LANES : LANES + NG, NG:] = part
    return jnp.asarray(forward, BF), jnp.asarray(inverse, BF)


def multiplier_parts():
    index = np.arange(NG)
    freq = np.where(index <= NG // 2, index, index - NG // 2).astype(np.float32)
    weight = (np.where((index == 0) | (index == NG // 2), 1.0, 2.0) / NG).astype(np.float32)
    pad = lambda v: np.pad(v, (0, LANES - NG))
    square = (freq**2).reshape(NG // 2, 2, 1) + pad(freq**2)
    scale = np.float32(KERNEL_SCALE) * weight.reshape(NG // 2, 2, 1) * pad(weight)
    wide = lambda v: np.broadcast_to(v[:, None], (NG, 2 * LANES))
    tall = lambda v: v.reshape(NG // 2, 2 * LANES)
    return [jnp.asarray(v, F32) for v in (wide(freq**2), wide(weight), tall(square), tall(scale))]


def multiplier_kernel(freq, weight, square, scale, out):
    for q in range(NG // 2):
        total = freq[...] + square[q : q + 1, :] + SCREEN_SQ
        out[q * NG : q * NG + NG, :] = weight[...] * scale[q : q + 1, :] / total


def multiplier():
    return pl.pallas_call(
        multiplier_kernel,
        out_shape=jax.ShapeDtypeStruct((NG // 2 * NG, 2 * LANES), F32),
        compiler_params=pltpu.CompilerParams(vmem_limit_bytes=SMALL_VMEM),
        name="multiplier",
    )(*multiplier_parts())


def dot(left, right):
    return jnp.dot(left, right, preferred_element_type=F32)


def pack_kernel(place, bands, for_a, for_b, b_keep, b_give, c_same, c_other):
    high, core = place[0], place[1]
    mix = high ^ core
    for p in range(bands.shape[1] // 2):
        packed = []
        for band in range(2):
            first, second = bands[band, 2 * p], bands[band, 2 * p + 1]
            heads = (first[:THIRD], first[THIRD:], second[:THIRD])
            rows = [
                jnp.concatenate([heads[g], second[THIRD:, 32 * g : 32 * g + 32]], axis=1)
                for g in range(3)
            ]
            packed.append(jnp.concatenate(rows, axis=0))
        pick = lambda flag: jnp.where(flag == 0, packed[0], packed[1]).astype(BF)
        for_a[0, p], for_a[1, p] = pick(core), pick(1 - core)
        mix_same, mix_other = pick(mix), pick(1 - mix)
        for_b[0, p], for_b[1, p] = mix_other, mix_same
        b_keep[p], b_give[p] = mix_same, mix_other
        c_same[p], c_other[p] = pick(high), pick(1 - high)


def one_slab(per):
    return pl.BlockSpec((per, ROWS, LANES), lambda i: (i, 0, 0))


def two_slabs(per):
    return pl.BlockSpec((2, per, ROWS, LANES), lambda i: (0, i, 0, 0))


def shape_of(count):
    dims = (PAIRS, ROWS, LANES)
    return jax.ShapeDtypeStruct(dims if count == 1 else (count, *dims), BF)


def pack(place, bands):
    steps = 3
    per = PAIRS // steps
    return pl.pallas_call(
        pack_kernel,
        grid=(steps,),
        in_specs=[
            pl.BlockSpec(memory_space=pltpu.SMEM),
            pl.BlockSpec((2, 2 * per, NG, NG), lambda i: (0, i, 0, 0)),
        ],
        out_specs=[two_slabs(per)] * 2 + [one_slab(per)] * 4,
        out_shape=[shape_of(2)] * 2 + [shape_of(1)] * 4,
        compiler_params=pltpu.CompilerParams(vmem_limit_bytes=SMALL_VMEM),
        name="pack",
    )(place, bands)


def unpack_kernel(place, a_same, a_cross, b_cross, b_own, b_mate, c_same, c_cross, out):
    high, core = place[0], place[1]
    mix = high ^ core
    for p in range(out.shape[1] // 2):
        load = lambda ref, *at: ref[(*at, p)].astype(F32)
        terms = (
            (core, load(a_same, 0) + load(a_cross, 0), load(a_same, 1) + load(a_cross, 1)),
            (mix, load(b_own) + load(b_cross, 1), load(b_mate, 0) + load(b_cross, 0)),
            (high, load(c_same), load(c_cross)),
        )
        for band in range(2):
            total = -sum(jnp.where(flag == band, same, other) for flag, same, other in terms)
            out[band, 2 * p] = total[: 2 * THIRD, :NG]
            tail = [total[THIRD * g : THIRD * g + THIRD, NG:] for g in range(3)]
            out[band, 2 * p + 1, :THIRD] = total[2 * THIRD :, :NG]
            out[band, 2 * p + 1, THIRD:] = jnp.concatenate(tail, axis=1)


def unpack(place, *parts):
    steps = 3
    per = PAIRS // steps
    specs = {3: one_slab(per), 4: two_slabs(per)}
    return pl.pallas_call(
        unpack_kernel,
        grid=(steps,),
        in_specs=[pl.BlockSpec(memory_space=pltpu.SMEM)] + [specs[v.ndim] for v in parts],
        out_specs=pl.BlockSpec((2, 2 * per, NG, NG), lambda i: (0, i, 0, 0)),
        out_shape=jax.ShapeDtypeStruct((2, 2 * PAIRS, NG, NG), F32),
        compiler_params=pltpu.CompilerParams(vmem_limit_bytes=SMALL_VMEM),
        name="unpack",
    )(place, *parts)


def transform(left, right, tables, grid_values, lines, emit):
    y_table, y_back, x_table, x_back, z_table, z_back, weights = tables
    flat = lambda v: v.reshape(-1, v.shape[-1])

    for r in range(4):
        held = lines.at[r % 2]

        def forward_z(i, carry, r=r, held=held):
            part = pl.ds(i * BATCH, BATCH)
            density = left[r][part] * right[r][part]
            sums = [
                dot(flat(density[:, THIRD * g : THIRD * g + THIRD]), z_table[g]) for g in range(3)
            ]
            tail = sums[0][:, LANES:] + sums[1][:, LANES:] + sums[2][:, LANES:]
            keep = lambda v: v.astype(BF).reshape(BATCH, THIRD, LANES)
            held[part, :THIRD, :LANES] = keep(sums[0][:, :LANES])
            held[part, THIRD:, :LANES] = keep(sums[1][:, :LANES])
            held[part, :THIRD, LANES:] = keep(sums[2][:, :LANES])
            held[part, THIRD:, LANES:] = keep(tail)
            return carry

        def forward_y(p, carry, r=r, held=held):
            values = dot(y_table[...], held[p])
            x = r * 2 * PAIRS + 2 * p
            grid_values[pl.ds(x, NG, stride=NG), :] = values[:, :LANES]
            grid_values[pl.ds(x + 1, NG, stride=NG), :] = values[:, LANES:]
            return carry

        lax.fori_loop(0, PAIRS // BATCH, forward_z, 0, unroll=True)
        lax.fori_loop(0, PAIRS, forward_y, 0, unroll=True)

    def middle(q, carry):
        upper = pl.ds(pl.multiple_of(q * 2 * NG, 2 * NG), NG)
        lower = pl.ds(pl.multiple_of(q * 2 * NG + NG, NG), NG)
        block = jnp.concatenate([grid_values[upper, :], grid_values[lower, :]], axis=1).astype(BF)
        scaled = weights[pl.ds(pl.multiple_of(q * NG, NG), NG), :] * dot(x_table[...], block)
        back = dot(x_back[...], scaled.astype(BF))
        grid_values[upper, :] = back[:, :LANES]
        grid_values[lower, :] = back[:, LANES:]
        return carry

    lax.fori_loop(0, NG // 2, middle, 0, unroll=16)

    for r in range(4):
        held = lines.at[r % 2]

        def inverse_y(p, carry, r=r, held=held):
            x = r * 2 * PAIRS + 2 * p
            one = grid_values[pl.ds(x, NG, stride=NG), :]
            two = grid_values[pl.ds(x + 1, NG, stride=NG), :]
            held[p] = dot(y_back[...], jnp.concatenate([one, two], axis=1).astype(BF)).astype(BF)
            return carry

        def inverse_z(i, carry, r=r, held=held):
            part = pl.ds(i * BATCH, BATCH)
            last = flat(held[part, THIRD:, LANES:])
            heads = (
                held[part, :THIRD, :LANES],
                held[part, THIRD:, :LANES],
                held[part, :THIRD, LANES:],
            )
            for g in range(3):
                values = dot(jnp.concatenate([flat(heads[g]), last], axis=1), z_back[g])
                at = (part, slice(THIRD * g, THIRD * g + THIRD))
                emit(r, at, values.astype(BF).reshape(BATCH, THIRD, LANES))
            return carry

        lax.fori_loop(0, PAIRS, inverse_y, 0, unroll=True)
        lax.fori_loop(0, PAIRS // BATCH, inverse_z, 0, unroll=True)


def whole(first, second, odd):
    part = lambda ref: ref if len(ref.shape) == 3 else ref.at[0]
    return [part(first), odd.at[0], part(second), odd.at[1]]


def first_kernel(*refs):
    c, b, refs = whole(*refs[7:10]), whole(*refs[10:13]), (*refs[:7], *refs[13:])
    field_cb, scratch = refs[7], refs[8:]

    def emit(r, at, potential):
        field_cb[(r, *at)] = potential

    transform(c, b, refs[:7], *scratch, emit)


def second_kernel(*refs):
    c, b, a = (whole(*refs[7 + 3 * n : 10 + 3 * n]) for n in range(3))
    field_cb, field_ca, c_keep, c_give = refs[16:20]
    out = (c_keep.at[0], c_give.at[0], c_keep.at[1], c_give.at[1])

    def emit(r, at, potential):
        field_ca[(r, *at)] = potential
        total = field_cb[(r, *at)].astype(F32) * b[r][at].astype(F32)
        out[r][at] = (total + potential.astype(F32) * a[r][at].astype(F32)).astype(BF)

    transform(c, a, refs[:7], *refs[20:], emit)


def third_kernel(*refs):
    c, b, a = (whole(*refs[7 + 3 * n : 10 + 3 * n]) for n in range(3))
    field_cb, field_ca, b_own, b_far, b_give, a_own, a_far, a_give = refs[16:24]
    out_b = (b_own, b_give.at[0], b_far, b_give.at[1])
    out_a = (a_own, a_give.at[0], a_far, a_give.at[1])

    def emit(r, at, potential):
        field = potential.astype(F32)
        one, two, three = (v[r][at].astype(F32) for v in (c, b, a))
        out_b[r][at] = (field_cb[(r, *at)].astype(F32) * one + field * three).astype(BF)
        out_a[r][at] = (field_ca[(r, *at)].astype(F32) * one + field * two).astype(BF)

    transform(b, a, refs[:7], *refs[24:], emit)


def call_transform(kernel, name, tables, slabs, outs):
    return pl.pallas_call(
        kernel,
        in_specs=[pl.BlockSpec(memory_space=pltpu.VMEM)] * (len(tables) + len(slabs)),
        out_specs=[pl.BlockSpec(memory_space=pltpu.VMEM)] * len(outs),
        out_shape=[shape_of(count) for count in outs],
        scratch_shapes=[
            pltpu.VMEM((NG * NG, LANES), F32),
            pltpu.VMEM((2, PAIRS, NG, 2 * LANES), BF),
        ],
        compiler_params=pltpu.CompilerParams(vmem_limit_bytes=LARGE_VMEM),
        cost_estimate=pl.CostEstimate(
            flops=1 << 20, bytes_accessed=1 << 16, transcendentals=0
        ),
        name=name,
    )(*tables, *slabs)


def sum_kernel(kept, received, same, cross):
    for n, out in enumerate((same, cross)):
        out[...] = (kept[n].astype(F32) + received[n].astype(F32)).astype(BF)


def add_halves(kept, received):
    return pl.pallas_call(
        sum_kernel,
        out_shape=[shape_of(1)] * 2,
        compiler_params=pltpu.CompilerParams(vmem_limit_bytes=SMALL_VMEM),
        name="add_halves",
    )(kept, received)


def passed(value, blocks, by, length):
    pairs = [
        (4 * k + s, 4 * ((k + by) % length) + (s ^ blocks)) for k in range(length) for s in range(4)
    ]
    return lax.ppermute(value, AXES, pairs)


def per_device(bands):
    length = lax.axis_size("band")
    me = lax.axis_index("grid")
    place = jnp.stack([me // 2, me % 2]).astype(jnp.int32)
    send = functools.partial(passed, length=length)

    for_a, for_b, b_keep, b_give, c_same, c_other = pack(place, bands)
    moved = lax.optimization_barrier(
        (
            send(c_same, 0, 2),
            send(c_other, 2, 2),
            send(for_b, 2, 0),
            send(for_a, 0, -1),
            send(for_a, 2, -1),
        )
    )
    c_same, c_cross, b_cross, a_same, a_cross = moved
    b = [b_keep, b_cross, send(jnp.stack([b_give, b_cross[1]]), 1, 0)]
    a = [a_same, a_cross, send(jnp.stack([a_same[1], a_cross[1]]), 1, 0)]
    c = [c_same, c_cross, send(jnp.stack([c_same, c_cross]), 1, 0)]

    table = dft_table(NG)
    orders = [np.concatenate([np.arange(24) + 24 * (r ^ s) for r in range(4)]) for s in range(4)]
    both = np.stack([np.stack([table[:, order], table[:, order].T]) for order in orders])
    x_table, x_back = lax.dynamic_index_in_dim(jnp.asarray(both, BF), me, 0, keepdims=False)
    y_table, y_back = jnp.asarray(table, BF), jnp.asarray(table.T, BF)
    tables = (y_table, y_back, x_table, x_back, *z_tables(), multiplier())

    (field_cb,) = call_transform(first_kernel, "pair_cb", tables, [*c, *b], [4])
    field_ca, c_keep, c_give = call_transform(
        second_kernel, "pair_ca", tables, [*c, *b, *a, field_cb], [4, 2, 2]
    )
    sums = add_halves(c_keep, send(c_give, 1, 0))
    c_same, c_cross, field_ca = lax.optimization_barrier((*sums, field_ca))
    c_same, c_cross = send(c_same, 0, -2), send(c_cross, 2, -2)
    b_own, b_far, b_give, a_own, a_far, a_give = call_transform(
        third_kernel, "pair_ba", tables, [*c, *b, *a, field_cb, field_ca], [1, 1, 2, 1, 1, 2]
    )
    a_mate, b_mate = send(a_give, 1, 0), send(b_give, 1, 0)
    a_same = send(jnp.stack([a_own, a_mate[0]]), 0, 1)
    a_cross = send(jnp.stack([a_far, a_mate[1]]), 2, 1)
    b_cross = send(jnp.stack([b_far, b_mate[1]]), 2, 0)
    return unpack(place, a_same, a_cross, b_cross, b_own, b_mate, c_same, c_cross)


def solution(mesh):
    spec = P("band", "grid", None, None)
    return jax.shard_map(
        per_device, mesh=mesh, in_specs=(spec,), out_specs=spec, check_vma=False
    )
```

```python
import functools

import jax
import jax.numpy as jnp
import numpy as np
from jax import lax
from jax.experimental import pallas as pl
from jax.experimental.pallas import tpu as pltpu
from jax.sharding import PartitionSpec as P


NG = 96
PAIRS = 12
ROWS = 144
THIRD = 48
LANES = 128
SLAB = PAIRS * ROWS
KERNEL_SCALE = 16.0
SCREEN_SQ = 0.05
AXES = ("band", "grid")
BF = jnp.bfloat16
F32 = jnp.float32
BATCH = 6
SMALL_VMEM = 24 << 20
LARGE_VMEM = 30 << 20


def dft_table(length):
    half = length // 2
    rows = np.arange(length)
    freq = np.where(rows <= half, rows, rows - half)
    phase = 2.0 * np.pi * np.outer(freq, rows) / length
    return np.where((rows <= half)[:, None], np.cos(phase), np.sin(phase))


def z_tables():
    table = dft_table(NG)
    forward = np.zeros((3, LANES, 2 * LANES))
    inverse = np.zeros((3, 2 * LANES, LANES))
    for g in range(3):
        part = table[:, 32 * g : 32 * g + 32]
        forward[g, :NG, :NG] = table.T
        forward[g, NG:, LANES : LANES + NG] = part.T
        inverse[g, :NG, :NG] = table
        inverse[g, LANES : LANES + NG, NG:] = part
    return jnp.asarray(forward, BF), jnp.asarray(inverse, BF)


def multiplier_parts():
    index = np.arange(NG)
    freq = np.where(index <= NG // 2, index, index - NG // 2).astype(np.float32)
    weight = (np.where((index == 0) | (index == NG // 2), 1.0, 2.0) / NG).astype(np.float32)
    pad = lambda v: np.pad(v, (0, LANES - NG))
    square = (freq**2).reshape(NG // 2, 2, 1) + pad(freq**2)
    scale = np.float32(KERNEL_SCALE) * weight.reshape(NG // 2, 2, 1) * pad(weight)
    wide = lambda v: np.broadcast_to(v[:, None], (NG, 2 * LANES))
    tall = lambda v: v.reshape(NG // 2, 2 * LANES)
    return [jnp.asarray(v, F32) for v in (wide(freq**2), wide(weight), tall(square), tall(scale))]


def multiplier_kernel(freq, weight, square, scale, out):
    for q in range(NG // 2):
        total = freq[...] + square[q : q + 1, :] + SCREEN_SQ
        out[q * NG : q * NG + NG, :] = weight[...] * scale[q : q + 1, :] / total


def multiplier():
    return pl.pallas_call(
        multiplier_kernel,
        out_shape=jax.ShapeDtypeStruct((NG // 2 * NG, 2 * LANES), F32),
        compiler_params=pltpu.CompilerParams(vmem_limit_bytes=SMALL_VMEM),
        name="multiplier",
    )(*multiplier_parts())


def dot(left, right):
    return jnp.dot(left, right, preferred_element_type=F32)


def pack_kernel(place, bands, both, b_keep, b_give, c_same):
    high, core = place[0], place[1]
    mix = high ^ core
    for p in range(bands.shape[1] // 2):
        packed = []
        for band in range(2):
            first, second = bands[band, 2 * p], bands[band, 2 * p + 1]
            heads = (first[:THIRD], first[THIRD:], second[:THIRD])
            rows = [
                jnp.concatenate([heads[g], second[THIRD:, 32 * g : 32 * g + 32]], axis=1)
                for g in range(3)
            ]
            packed.append(jnp.concatenate(rows, axis=0))
        pick = lambda flag: jnp.where(flag == 0, packed[0], packed[1]).astype(BF)
        both[0, p], both[1, p] = pick(core), pick(1 - core)
        b_keep[p], b_give[p] = pick(mix), pick(1 - mix)
        c_same[p] = pick(high)


def one_slab(per):
    return pl.BlockSpec((per, ROWS, LANES), lambda i: (i, 0, 0))


def two_slabs(per):
    return pl.BlockSpec((2, per, ROWS, LANES), lambda i: (0, i, 0, 0))


def shape_of(count):
    dims = (PAIRS, ROWS, LANES)
    return jax.ShapeDtypeStruct(dims if count == 1 else (count, *dims), BF)


def pack(place, bands):
    steps = 3
    per = PAIRS // steps
    return pl.pallas_call(
        pack_kernel,
        grid=(steps,),
        in_specs=[
            pl.BlockSpec(memory_space=pltpu.SMEM),
            pl.BlockSpec((2, 2 * per, NG, NG), lambda i: (0, i, 0, 0)),
        ],
        out_specs=[two_slabs(per)] + [one_slab(per)] * 3,
        out_shape=[shape_of(2)] + [shape_of(1)] * 3,
        compiler_params=pltpu.CompilerParams(vmem_limit_bytes=SMALL_VMEM),
        name="pack",
    )(place, bands)


def unpack_kernel(place, a_same, a_cross, b_cross, b_own, b_mate, c_same, c_cross, out):
    high, core = place[0], place[1]
    mix = high ^ core
    for p in range(out.shape[1] // 2):
        load = lambda ref, *at: ref[(*at, p)].astype(F32)
        terms = (
            (core, load(a_same, 0) + load(a_cross, 0), load(a_same, 1) + load(a_cross, 1)),
            (mix, load(b_own) + load(b_cross, 1), load(b_mate, 0) + load(b_cross, 0)),
            (high, load(c_same), load(c_cross)),
        )
        for band in range(2):
            total = -sum(jnp.where(flag == band, same, other) for flag, same, other in terms)
            out[band, 2 * p] = total[: 2 * THIRD, :NG]
            tail = [total[THIRD * g : THIRD * g + THIRD, NG:] for g in range(3)]
            out[band, 2 * p + 1, :THIRD] = total[2 * THIRD :, :NG]
            out[band, 2 * p + 1, THIRD:] = jnp.concatenate(tail, axis=1)


def unpack(place, *parts):
    steps = 3
    per = PAIRS // steps
    specs = {3: one_slab(per), 4: two_slabs(per)}
    return pl.pallas_call(
        unpack_kernel,
        grid=(steps,),
        in_specs=[pl.BlockSpec(memory_space=pltpu.SMEM)] + [specs[v.ndim] for v in parts],
        out_specs=pl.BlockSpec((2, 2 * per, NG, NG), lambda i: (0, i, 0, 0)),
        out_shape=jax.ShapeDtypeStruct((2, 2 * PAIRS, NG, NG), F32),
        compiler_params=pltpu.CompilerParams(vmem_limit_bytes=SMALL_VMEM),
        name="unpack",
    )(place, *parts)


def transform(left, right, tables, grid_values, lines, emit):
    y_table, y_back, x_table, x_back, z_table, z_back, weights = tables
    flat = lambda v: v.reshape(-1, v.shape[-1])

    for r in range(4):
        held = lines.at[r % 2]

        def forward_z(i, carry, r=r, held=held):
            part = pl.ds(i * BATCH, BATCH)
            density = left[r][part] * right[r][part]
            sums = [
                dot(flat(density[:, THIRD * g : THIRD * g + THIRD]), z_table[g]) for g in range(3)
            ]
            tail = sums[0][:, LANES:] + sums[1][:, LANES:] + sums[2][:, LANES:]
            keep = lambda v: v.astype(BF).reshape(BATCH, THIRD, LANES)
            held[part, :THIRD, :LANES] = keep(sums[0][:, :LANES])
            held[part, THIRD:, :LANES] = keep(sums[1][:, :LANES])
            held[part, :THIRD, LANES:] = keep(sums[2][:, :LANES])
            held[part, THIRD:, LANES:] = keep(tail)
            return carry

        def forward_y(p, carry, r=r, held=held):
            values = dot(y_table[...], held[p])
            x = r * 2 * PAIRS + 2 * p
            grid_values[pl.ds(x, NG, stride=NG), :] = values[:, :LANES]
            grid_values[pl.ds(x + 1, NG, stride=NG), :] = values[:, LANES:]
            return carry

        lax.fori_loop(0, PAIRS // BATCH, forward_z, 0, unroll=True)
        lax.fori_loop(0, PAIRS, forward_y, 0, unroll=True)

    def middle(q, carry):
        upper = pl.ds(pl.multiple_of(q * 2 * NG, 2 * NG), NG)
        lower = pl.ds(pl.multiple_of(q * 2 * NG + NG, NG), NG)
        block = jnp.concatenate([grid_values[upper, :], grid_values[lower, :]], axis=1).astype(BF)
        scaled = weights[pl.ds(pl.multiple_of(q * NG, NG), NG), :] * dot(x_table[...], block)
        back = dot(x_back[...], scaled.astype(BF))
        grid_values[upper, :] = back[:, :LANES]
        grid_values[lower, :] = back[:, LANES:]
        return carry

    lax.fori_loop(0, NG // 2, middle, 0, unroll=16)

    for r in range(4):
        held = lines.at[r % 2]

        def inverse_y(p, carry, r=r, held=held):
            x = r * 2 * PAIRS + 2 * p
            one = grid_values[pl.ds(x, NG, stride=NG), :]
            two = grid_values[pl.ds(x + 1, NG, stride=NG), :]
            held[p] = dot(y_back[...], jnp.concatenate([one, two], axis=1).astype(BF)).astype(BF)
            return carry

        def inverse_z(i, carry, r=r, held=held):
            part = pl.ds(i * BATCH, BATCH)
            last = flat(held[part, THIRD:, LANES:])
            heads = (
                held[part, :THIRD, :LANES],
                held[part, THIRD:, :LANES],
                held[part, :THIRD, LANES:],
            )
            for g in range(3):
                values = dot(jnp.concatenate([flat(heads[g]), last], axis=1), z_back[g])
                at = (part, slice(THIRD * g, THIRD * g + THIRD))
                emit(r, at, values.astype(BF).reshape(BATCH, THIRD, LANES))
            return carry

        lax.fori_loop(0, PAIRS, inverse_y, 0, unroll=True)
        lax.fori_loop(0, PAIRS // BATCH, inverse_z, 0, unroll=True)


def slabs_of(refs, count):
    parts = [ref if len(ref.shape) == 3 else ref.at[0] for ref in refs[: 4 * count]]
    return [parts[4 * n : 4 * n + 4] for n in range(count)]


def first_kernel(*refs):
    a, b = slabs_of(refs[7:], 2)
    field_ab, scratch = refs[15], refs[16:]

    def emit(r, at, potential):
        field_ab[(r, *at)] = potential

    transform(a, b, refs[:7], *scratch, emit)


def second_kernel(*refs):
    a, b, c = slabs_of(refs[7:], 3)
    field_ab, field_ac, a_own, a_far, a_give = refs[19:24]
    out = (a_own, a_give.at[0], a_far, a_give.at[1])

    def emit(r, at, potential):
        field_ac[(r, *at)] = potential
        total = field_ab[(r, *at)].astype(F32) * b[r][at].astype(F32)
        out[r][at] = (total + potential.astype(F32) * c[r][at].astype(F32)).astype(BF)

    transform(a, c, refs[:7], *refs[24:], emit)


def third_kernel(*refs):
    a, b, c = slabs_of(refs[7:], 3)
    field_ab, field_ac, b_own, b_far, b_give, c_keep, c_give = refs[19:26]
    out_b = (b_own, b_give.at[0], b_far, b_give.at[1])
    out_c = (c_keep.at[0], c_give.at[0], c_keep.at[1], c_give.at[1])

    def emit(r, at, potential):
        field = potential.astype(F32)
        one, two, three = (v[r][at].astype(F32) for v in (a, b, c))
        out_b[r][at] = (field_ab[(r, *at)].astype(F32) * one + field * three).astype(BF)
        out_c[r][at] = (field_ac[(r, *at)].astype(F32) * one + field * two).astype(BF)

    transform(b, c, refs[:7], *refs[26:], emit)


def call_transform(kernel, name, tables, slabs, outs):
    return pl.pallas_call(
        kernel,
        in_specs=[pl.BlockSpec(memory_space=pltpu.VMEM)] * (len(tables) + len(slabs)),
        out_specs=[pl.BlockSpec(memory_space=pltpu.VMEM)] * len(outs),
        out_shape=[shape_of(count) for count in outs],
        scratch_shapes=[
            pltpu.VMEM((NG * NG, LANES), F32),
            pltpu.VMEM((2, PAIRS, NG, 2 * LANES), BF),
        ],
        compiler_params=pltpu.CompilerParams(vmem_limit_bytes=LARGE_VMEM),
        cost_estimate=pl.CostEstimate(
            flops=1 << 20, bytes_accessed=1 << 16, transcendentals=0
        ),
        name=name,
    )(*tables, *slabs)


def sum_kernel(kept, received, same, cross):
    for n, out in enumerate((same, cross)):
        out[...] = (kept[n].astype(F32) + received[n].astype(F32)).astype(BF)


def add_halves(kept, received):
    return pl.pallas_call(
        sum_kernel,
        out_shape=[shape_of(1)] * 2,
        compiler_params=pltpu.CompilerParams(vmem_limit_bytes=SMALL_VMEM),
        name="add_halves",
    )(kept, received)


def passed(value, blocks, by, length):
    pairs = [
        (4 * k + s, 4 * ((k + by) % length) + (s ^ blocks)) for k in range(length) for s in range(4)
    ]
    return lax.ppermute(value, AXES, pairs)


def per_device(bands):
    length = lax.axis_size("band")
    me = lax.axis_index("grid")
    place = jnp.stack([me // 2, me % 2]).astype(jnp.int32)
    send = functools.partial(passed, length=length)

    table = dft_table(NG)
    orders = [np.concatenate([np.arange(24) + 24 * (r ^ s) for r in range(4)]) for s in range(4)]
    tabled = np.stack([np.stack([table[:, order], table[:, order].T]) for order in orders])
    x_tables = lax.dynamic_index_in_dim(jnp.asarray(tabled, BF), me, 0, keepdims=False)
    weights = multiplier()

    both, b_keep, b_give, c_near = pack(place, bands)
    b_far, a_near, c_near = send(both, 2, 0), send(both, 0, -1), send(c_near, 0, 2)
    b_mate = send(b_give, 1, 0)
    b_far, a_near, c_near, b_mate, x_tables, weights = lax.optimization_barrier(
        (b_far, a_near, c_near, b_mate, x_tables, weights)
    )
    pick = lambda pair, index: lax.dynamic_index_in_dim(pair, index, 0, keepdims=False)
    a_far = send(b_far, 0, -1)
    c_far = send(pick(b_far, place[0] ^ place[1]), 0, 2)
    b = [b_keep, b_mate, pick(b_far, place[0]), send(pick(b_far, 1 - place[0]), 1, 0)]
    a_mate, c_mate = send(a_near[1], 1, 0), send(c_near, 1, 0)
    a_far, c_far, a_mate, c_mate, b = lax.optimization_barrier((a_far, c_far, a_mate, c_mate, b))
    c = [c_near, c_mate, c_far, send(c_far, 1, 0)]
    a = [a_near, a_mate, a_far, send(a_far[1], 1, 0)]

    y_table, y_back = jnp.asarray(table, BF), jnp.asarray(table.T, BF)
    tables = (y_table, y_back, x_tables[0], x_tables[1], *z_tables(), weights)
    (field_ab,) = call_transform(first_kernel, "pair_ab", tables, [*a, *b], [4])
    field_ac, a_own, a_far, a_give = call_transform(
        second_kernel, "pair_ac", tables, [*a, *b, *c, field_ab], [4, 1, 1, 2]
    )
    a_mate = send(a_give, 1, 0)
    a_same, a_cross = jnp.stack([a_own, a_mate[0]]), jnp.stack([a_far, a_mate[1]])
    a_same, a_cross, field_ac = lax.optimization_barrier((a_same, a_cross, field_ac))
    a_same, a_cross = send(a_same, 0, 1), send(a_cross, 2, 1)
    b_own, b_far, b_give, c_keep, c_give = call_transform(
        third_kernel, "pair_bc", tables, [*a, *b, *c, field_ab, field_ac], [1, 1, 2, 2, 2]
    )
    c_same, c_cross = add_halves(c_keep, send(c_give, 1, 0))
    c_same, c_cross = send(c_same, 0, -2), send(c_cross, 2, -2)
    b_mate = send(b_give, 1, 0)
    b_cross = send(jnp.stack([b_far, b_mate[1]]), 2, 0)
    return unpack(place, a_same, a_cross, b_cross, b_own, b_mate, c_same, c_cross)


def solution(mesh):
    spec = P("band", "grid", None, None)
    return jax.shard_map(
        per_device, mesh=mesh, in_specs=(spec,), out_specs=spec, check_vma=False
    )
```

```python
import functools

import jax
import jax.numpy as jnp
import numpy as np
from jax import lax
from jax.experimental import pallas as pl
from jax.experimental.pallas import tpu as pltpu
from jax.sharding import PartitionSpec as P


NG = 96
PAIRS = 12
ROWS = 144
THIRD = 48
LANES = 128
SLAB = PAIRS * ROWS
KERNEL_SCALE = 16.0
SCREEN_SQ = 0.05
AXES = ("band", "grid")
BF = jnp.bfloat16
F32 = jnp.float32
BATCH = 6
FIRST = 12 * 100 * NG**4
SMALL_VMEM = 24 << 20
LARGE_VMEM = 30 << 20


def dft_table(length):
    half = length // 2
    rows = np.arange(length)
    freq = np.where(rows <= half, rows, rows - half)
    phase = 2.0 * np.pi * np.outer(freq, rows) / length
    return np.where((rows <= half)[:, None], np.cos(phase), np.sin(phase))


def z_tables():
    table = dft_table(NG)
    forward = np.zeros((3, LANES, 2 * LANES))
    inverse = np.zeros((3, 2 * LANES, LANES))
    for g in range(3):
        part = table[:, 32 * g : 32 * g + 32]
        forward[g, :NG, :NG] = table.T
        forward[g, NG:, LANES : LANES + NG] = part.T
        inverse[g, :NG, :NG] = table
        inverse[g, LANES : LANES + NG, NG:] = part
    return jnp.asarray(forward, BF), jnp.asarray(inverse, BF)


def frequency_weights(rows):
    freq = jnp.where(rows <= NG // 2, rows, rows - NG // 2).astype(F32)
    weight = jnp.where((rows == 0) | (rows == NG // 2), 1.0, 2.0) / NG
    return freq * freq, jnp.where(rows < NG, weight, 0.0)


def multiplier_kernel(out):
    dims = (NG, 2 * LANES)
    lane = lax.broadcasted_iota(jnp.int32, dims, 1)
    square_a, weight_a = frequency_weights(lax.broadcasted_iota(jnp.int32, dims, 0))
    square_c, weight_c = frequency_weights(lane % LANES)
    square = square_a + square_c + SCREEN_SQ
    scale = KERNEL_SCALE * weight_a * weight_c
    for q in range(NG // 2):
        even, odd = (frequency_weights(jnp.int32(2 * q + n)) for n in range(2))
        square_b, weight_b = (jnp.where(lane < LANES, *pair) for pair in zip(even, odd))
        out[q * NG : q * NG + NG, :] = scale * weight_b / (square + square_b)


def multiplier():
    return pl.pallas_call(
        multiplier_kernel,
        out_shape=jax.ShapeDtypeStruct((NG // 2 * NG, 2 * LANES), F32),
        compiler_params=pltpu.CompilerParams(vmem_limit_bytes=SMALL_VMEM),
        name="multiplier",
    )()


def dot(left, right):
    return jnp.dot(left, right, preferred_element_type=F32)


def pack_kernel(place, bands, for_a, for_b, b_keep, b_give, c_same, c_other):
    high, core = place[0], place[1]
    mix = high ^ core
    for p in range(bands.shape[1] // 2):
        packed = []
        for band in range(2):
            first, second = bands[band, 2 * p], bands[band, 2 * p + 1]
            heads = (first[:THIRD], first[THIRD:], second[:THIRD])
            rows = [
                jnp.concatenate([heads[g], second[THIRD:, 32 * g : 32 * g + 32]], axis=1)
                for g in range(3)
            ]
            packed.append(jnp.concatenate(rows, axis=0))
        pick = lambda flag: jnp.where(flag == 0, packed[0], packed[1]).astype(BF)
        for_a[0, p], for_a[1, p] = pick(core), pick(1 - core)
        mix_same, mix_other = pick(mix), pick(1 - mix)
        for_b[0, p], for_b[1, p] = mix_other, mix_same
        b_keep[p], b_give[p] = mix_same, mix_other
        c_same[p], c_other[p] = pick(high), pick(1 - high)


def one_slab(per):
    return pl.BlockSpec((per, ROWS, LANES), lambda i: (i, 0, 0))


def two_slabs(per):
    return pl.BlockSpec((2, per, ROWS, LANES), lambda i: (0, i, 0, 0))


def shape_of(count):
    dims = (PAIRS, ROWS, LANES)
    return jax.ShapeDtypeStruct(dims if count == 1 else (count, *dims), BF)


def pack(place, bands):
    steps = 3
    per = PAIRS // steps
    return pl.pallas_call(
        pack_kernel,
        grid=(steps,),
        in_specs=[
            pl.BlockSpec(memory_space=pltpu.SMEM),
            pl.BlockSpec((2, 2 * per, NG, NG), lambda i: (0, i, 0, 0)),
        ],
        out_specs=[two_slabs(per)] * 2 + [one_slab(per)] * 4,
        out_shape=[shape_of(2)] * 2 + [shape_of(1)] * 4,
        compiler_params=pltpu.CompilerParams(vmem_limit_bytes=SMALL_VMEM),
        name="pack",
    )(place, bands)


def unpack_kernel(place, a_same, a_cross, b_cross, b_own, b_mate, c_same, c_cross, out):
    high, core = place[0], place[1]
    mix = high ^ core
    for p in range(out.shape[1] // 2):
        load = lambda ref, *at: ref[(*at, p)].astype(F32)
        terms = (
            (core, load(a_same, 0) + load(a_cross, 0), load(a_same, 1) + load(a_cross, 1)),
            (mix, load(b_own) + load(b_cross, 1), load(b_mate, 0) + load(b_cross, 0)),
            (high, load(c_same), load(c_cross)),
        )
        for band in range(2):
            total = -sum(jnp.where(flag == band, same, other) for flag, same, other in terms)
            out[band, 2 * p] = total[: 2 * THIRD, :NG]
            tail = [total[THIRD * g : THIRD * g + THIRD, NG:] for g in range(3)]
            out[band, 2 * p + 1, :THIRD] = total[2 * THIRD :, :NG]
            out[band, 2 * p + 1, THIRD:] = jnp.concatenate(tail, axis=1)


def unpack(place, *parts):
    steps = 3
    per = PAIRS // steps
    specs = {3: one_slab(per), 4: two_slabs(per)}
    return pl.pallas_call(
        unpack_kernel,
        grid=(steps,),
        in_specs=[pl.BlockSpec(memory_space=pltpu.SMEM)] + [specs[v.ndim] for v in parts],
        out_specs=pl.BlockSpec((2, 2 * per, NG, NG), lambda i: (0, i, 0, 0)),
        out_shape=jax.ShapeDtypeStruct((2, 2 * PAIRS, NG, NG), F32),
        compiler_params=pltpu.CompilerParams(vmem_limit_bytes=SMALL_VMEM),
        name="unpack",
    )(place, *parts)


def transform(left, right, tables, grid_values, lines, emit):
    y_table, y_back, x_table, x_back, z_table, z_back, weights = tables
    flat = lambda v: v.reshape(-1, v.shape[-1])

    for r in range(4):
        held = lines.at[r % 2]

        def forward_z(i, carry, r=r, held=held):
            part = pl.ds(i * BATCH, BATCH)
            density = left[r][part] * right[r][part]
            sums = [
                dot(flat(density[:, THIRD * g : THIRD * g + THIRD]), z_table[g]) for g in range(3)
            ]
            tail = sums[0][:, LANES:] + sums[1][:, LANES:] + sums[2][:, LANES:]
            keep = lambda v: v.astype(BF).reshape(BATCH, THIRD, LANES)
            held[part, :THIRD, :LANES] = keep(sums[0][:, :LANES])
            held[part, THIRD:, :LANES] = keep(sums[1][:, :LANES])
            held[part, :THIRD, LANES:] = keep(sums[2][:, :LANES])
            held[part, THIRD:, LANES:] = keep(tail)
            return carry

        def forward_y(p, carry, r=r, held=held):
            values = dot(y_table[...], held[p])
            x = r * 2 * PAIRS + 2 * p
            grid_values[pl.ds(x, NG, stride=NG), :] = values[:, :LANES]
            grid_values[pl.ds(x + 1, NG, stride=NG), :] = values[:, LANES:]
            return carry

        lax.fori_loop(0, PAIRS // BATCH, forward_z, 0, unroll=True)
        lax.fori_loop(0, PAIRS, forward_y, 0, unroll=True)

    def middle(q, carry):
        upper = pl.ds(pl.multiple_of(q * 2 * NG, 2 * NG), NG)
        lower = pl.ds(pl.multiple_of(q * 2 * NG + NG, NG), NG)
        block = jnp.concatenate([grid_values[upper, :], grid_values[lower, :]], axis=1).astype(BF)
        scaled = weights[pl.ds(pl.multiple_of(q * NG, NG), NG), :] * dot(x_table[...], block)
        back = dot(x_back[...], scaled.astype(BF))
        grid_values[upper, :] = back[:, :LANES]
        grid_values[lower, :] = back[:, LANES:]
        return carry

    lax.fori_loop(0, NG // 2, middle, 0, unroll=16)

    for r in range(4):
        held = lines.at[r % 2]

        def inverse_y(p, carry, r=r, held=held):
            x = r * 2 * PAIRS + 2 * p
            one = grid_values[pl.ds(x, NG, stride=NG), :]
            two = grid_values[pl.ds(x + 1, NG, stride=NG), :]
            held[p] = dot(y_back[...], jnp.concatenate([one, two], axis=1).astype(BF)).astype(BF)
            return carry

        def inverse_z(i, carry, r=r, held=held):
            part = pl.ds(i * BATCH, BATCH)
            last = flat(held[part, THIRD:, LANES:])
            heads = (
                held[part, :THIRD, :LANES],
                held[part, THIRD:, :LANES],
                held[part, :THIRD, LANES:],
            )
            for g in range(3):
                values = dot(jnp.concatenate([flat(heads[g]), last], axis=1), z_back[g])
                at = (part, slice(THIRD * g, THIRD * g + THIRD))
                emit(r, at, values.astype(BF).reshape(BATCH, THIRD, LANES))
            return carry

        lax.fori_loop(0, PAIRS, inverse_y, 0, unroll=True)
        lax.fori_loop(0, PAIRS // BATCH, inverse_z, 0, unroll=True)


def slabs_of(refs, count):
    part = lambda ref: ref if len(ref.shape) == 3 else ref.at[0]
    groups = [refs[3 * n : 3 * n + 3] for n in range(count)]
    return [[part(one), odd.at[0], part(two), odd.at[1]] for one, two, odd in groups]


def first_kernel(*refs):
    a, b = slabs_of(refs[7:], 2)
    field_ab, scratch = refs[13], refs[14:]

    def emit(r, at, potential):
        field_ab[(r, *at)] = potential

    transform(a, b, refs[:7], *scratch, emit)


def second_kernel(*refs):
    a, b, c = slabs_of(refs[7:], 3)
    field_ab, field_ac, a_own, a_far, a_give = refs[16:21]
    out = (a_own, a_give.at[0], a_far, a_give.at[1])

    def emit(r, at, potential):
        field_ac[(r, *at)] = potential
        total = field_ab[(r, *at)].astype(F32) * b[r][at].astype(F32)
        out[r][at] = (total + potential.astype(F32) * c[r][at].astype(F32)).astype(BF)

    transform(a, c, refs[:7], *refs[21:], emit)


def third_kernel(*refs):
    a, b, c = slabs_of(refs[7:], 3)
    field_ab, field_ac, b_own, b_far, b_give, c_keep, c_give = refs[16:23]
    out_b = (b_own, b_give.at[0], b_far, b_give.at[1])
    out_c = (c_keep.at[0], c_give.at[0], c_keep.at[1], c_give.at[1])

    def emit(r, at, potential):
        field = potential.astype(F32)
        one, two, three = (v[r][at].astype(F32) for v in (a, b, c))
        out_b[r][at] = (field_ab[(r, *at)].astype(F32) * one + field * three).astype(BF)
        out_c[r][at] = (field_ac[(r, *at)].astype(F32) * one + field * two).astype(BF)

    transform(b, c, refs[:7], *refs[23:], emit)


def call_transform(kernel, name, tables, slabs, outs, flops=12 * 10 * NG**4):
    return pl.pallas_call(
        kernel,
        in_specs=[pl.BlockSpec(memory_space=pltpu.VMEM)] * (len(tables) + len(slabs)),
        out_specs=[pl.BlockSpec(memory_space=pltpu.VMEM)] * len(outs),
        out_shape=[shape_of(count) for count in outs],
        scratch_shapes=[
            pltpu.VMEM((NG * NG, LANES), F32),
            pltpu.VMEM((2, PAIRS, NG, 2 * LANES), BF),
        ],
        compiler_params=pltpu.CompilerParams(vmem_limit_bytes=LARGE_VMEM),
        cost_estimate=pl.CostEstimate(
            flops=flops, bytes_accessed=1 << 16, transcendentals=0
        ),
        name=name,
    )(*tables, *slabs)


def sum_kernel(kept, received, same, cross):
    for n, out in enumerate((same, cross)):
        out[...] = (kept[n].astype(F32) + received[n].astype(F32)).astype(BF)


def add_halves(kept, received):
    return pl.pallas_call(
        sum_kernel,
        out_shape=[shape_of(1)] * 2,
        compiler_params=pltpu.CompilerParams(vmem_limit_bytes=SMALL_VMEM),
        name="add_halves",
    )(kept, received)


def passed(value, blocks, by, length):
    pairs = [
        (4 * k + s, 4 * ((k + by) % length) + (s ^ blocks)) for k in range(length) for s in range(4)
    ]
    return lax.ppermute(value, AXES, pairs)


def per_device(bands):
    length = lax.axis_size("band")
    me = lax.axis_index("grid")
    place = jnp.stack([me // 2, me % 2]).astype(jnp.int32)
    send = functools.partial(passed, length=length)

    table = dft_table(NG)
    orders = [np.concatenate([np.arange(24) + 24 * (r ^ s) for r in range(4)]) for s in range(4)]
    both = np.stack([np.stack([table[:, order], table[:, order].T]) for order in orders])
    x_tables = lax.dynamic_index_in_dim(jnp.asarray(both, BF), me, 0, keepdims=False)

    for_a, for_b, b_keep, b_give, c_same, c_other = pack(place, bands)
    moved = (
        send(c_same, 0, 2),
        send(c_other, 2, 2),
        send(for_b, 2, 0),
        send(for_a, 0, -1),
        send(for_a, 2, -1),
    )
    moved, x_tables = lax.optimization_barrier((moved, x_tables))
    c_same, c_cross, b_cross, a_same, a_cross = moved
    b = [b_keep, b_cross, send(jnp.stack([b_give, b_cross[1]]), 1, 0)]
    a = [a_same, a_cross, send(jnp.stack([a_same[1], a_cross[1]]), 1, 0)]

    y_table, y_back = jnp.asarray(table, BF), jnp.asarray(table.T, BF)
    tables = (y_table, y_back, x_tables[0], x_tables[1], *z_tables(), multiplier())
    (field_ab,) = call_transform(first_kernel, "pair_ab", tables, [*a, *b], [4], FIRST)
    c = [c_same, c_cross, send(jnp.stack([c_same, c_cross]), 1, 0)]
    field_ac, a_own, a_far, a_give = call_transform(
        second_kernel, "pair_ac", tables, [*a, *b, *c, field_ab], [4, 1, 1, 2]
    )
    a_mate = send(a_give, 1, 0)
    a_same, a_cross = jnp.stack([a_own, a_mate[0]]), jnp.stack([a_far, a_mate[1]])
    a_same, a_cross, field_ac = lax.optimization_barrier((a_same, a_cross, field_ac))
    b_own, b_far, b_give, c_keep, c_give = call_transform(
        third_kernel, "pair_bc", tables, [*a, *b, *c, field_ab, field_ac], [1, 1, 2, 2, 2]
    )
    sums = add_halves(c_keep, send(c_give, 1, 0))
    c_same, c_cross, a_same, a_cross = lax.optimization_barrier((*sums, a_same, a_cross))
    c_same, c_cross = send(c_same, 0, -1), send(c_cross, 2, -1)
    c_same, c_cross = send(c_same, 0, -1), send(c_cross, 0, -1)
    a_same, a_cross = send(a_same, 0, 1), send(a_cross, 2, 1)
    b_mate = send(b_give, 1, 0)
    b_cross = send(jnp.stack([b_far, b_mate[1]]), 2, 0)
    return unpack(place, a_same, a_cross, b_cross, b_own, b_mate, c_same, c_cross)


def solution(mesh):
    spec = P("band", "grid", None, None)
    return jax.shard_map(
        per_device, mesh=mesh, in_specs=(spec,), out_specs=spec, check_vma=False
    )
```

```python
import functools

import jax
import jax.numpy as jnp
import numpy as np
from jax import lax
from jax.experimental import pallas as pl
from jax.experimental.pallas import tpu as pltpu
from jax.sharding import PartitionSpec as P


NG = 96
PAIRS = 12
ROWS = 144
THIRD = 48
LANES = 128
SLAB = PAIRS * ROWS
KERNEL_SCALE = 16.0
SCREEN_SQ = 0.05
AXES = ("band", "grid")
BF = jnp.bfloat16
F32 = jnp.float32
BATCH = 6
FIRST = 12 * 100 * NG**4
SMALL_VMEM = 24 << 20
LARGE_VMEM = 30 << 20


def dft_table(length):
    half = length // 2
    rows = np.arange(length)
    freq = np.where(rows <= half, rows, rows - half)
    phase = 2.0 * np.pi * np.outer(freq, rows) / length
    return np.where((rows <= half)[:, None], np.cos(phase), np.sin(phase))


def z_tables():
    table = dft_table(NG)
    forward = np.zeros((3, LANES, 2 * LANES))
    inverse = np.zeros((3, 2 * LANES, LANES))
    for g in range(3):
        part = table[:, 32 * g : 32 * g + 32]
        forward[g, :NG, :NG] = table.T
        forward[g, NG:, LANES : LANES + NG] = part.T
        inverse[g, :NG, :NG] = table
        inverse[g, LANES : LANES + NG, NG:] = part
    return jnp.asarray(forward, BF), jnp.asarray(inverse, BF)


def frequency_weights(rows):
    freq = jnp.where(rows <= NG // 2, rows, rows - NG // 2).astype(F32)
    weight = jnp.where((rows == 0) | (rows == NG // 2), 1.0, 2.0) / NG
    return freq * freq, jnp.where(rows < NG, weight, 0.0)


def multiplier_kernel(out):
    dims = (NG, 2 * LANES)
    lane = lax.broadcasted_iota(jnp.int32, dims, 1)
    square_a, weight_a = frequency_weights(lax.broadcasted_iota(jnp.int32, dims, 0))
    square_c, weight_c = frequency_weights(lane % LANES)
    square = square_a + square_c + SCREEN_SQ
    scale = KERNEL_SCALE * weight_a * weight_c
    for q in range(NG // 2):
        even, odd = (frequency_weights(jnp.int32(2 * q + n)) for n in range(2))
        square_b, weight_b = (jnp.where(lane < LANES, *pair) for pair in zip(even, odd))
        out[q * NG : q * NG + NG, :] = scale * weight_b / (square + square_b)


def multiplier():
    return pl.pallas_call(
        multiplier_kernel,
        out_shape=jax.ShapeDtypeStruct((NG // 2 * NG, 2 * LANES), F32),
        compiler_params=pltpu.CompilerParams(vmem_limit_bytes=SMALL_VMEM),
        name="multiplier",
    )()


def dot(left, right):
    return jnp.dot(left, right, preferred_element_type=F32)


def pack_kernel(place, bands, for_a, for_b, b_keep, b_give, c_same, c_other):
    high, core = place[0], place[1]
    mix = high ^ core
    for p in range(bands.shape[1] // 2):
        packed = []
        for band in range(2):
            first, second = bands[band, 2 * p], bands[band, 2 * p + 1]
            heads = (first[:THIRD], first[THIRD:], second[:THIRD])
            rows = [
                jnp.concatenate([heads[g], second[THIRD:, 32 * g : 32 * g + 32]], axis=1)
                for g in range(3)
            ]
            packed.append(jnp.concatenate(rows, axis=0))
        pick = lambda flag: jnp.where(flag == 0, packed[0], packed[1]).astype(BF)
        for_a[0, p], for_a[1, p] = pick(core), pick(1 - core)
        mix_same, mix_other = pick(mix), pick(1 - mix)
        for_b[0, p], for_b[1, p] = mix_other, mix_same
        b_keep[p], b_give[p] = mix_same, mix_other
        c_same[p], c_other[p] = pick(high), pick(1 - high)


def one_slab(per):
    return pl.BlockSpec((per, ROWS, LANES), lambda i: (i, 0, 0))


def two_slabs(per):
    return pl.BlockSpec((2, per, ROWS, LANES), lambda i: (0, i, 0, 0))


def shape_of(count):
    dims = (PAIRS, ROWS, LANES)
    return jax.ShapeDtypeStruct(dims if count == 1 else (count, *dims), BF)


def pack(place, bands):
    steps = 3
    per = PAIRS // steps
    return pl.pallas_call(
        pack_kernel,
        grid=(steps,),
        in_specs=[
            pl.BlockSpec(memory_space=pltpu.SMEM),
            pl.BlockSpec((2, 2 * per, NG, NG), lambda i: (0, i, 0, 0)),
        ],
        out_specs=[two_slabs(per)] * 2 + [one_slab(per)] * 4,
        out_shape=[shape_of(2)] * 2 + [shape_of(1)] * 4,
        compiler_params=pltpu.CompilerParams(vmem_limit_bytes=SMALL_VMEM),
        name="pack",
    )(place, bands)


def unpack_kernel(place, a_same, a_cross, b_cross, b_own, b_mate, c_same, c_cross, out):
    high, core = place[0], place[1]
    mix = high ^ core
    for p in range(out.shape[1] // 2):
        load = lambda ref, *at: ref[(*at, p)].astype(F32)
        terms = (
            (core, load(a_same, 0) + load(a_cross, 0), load(a_same, 1) + load(a_cross, 1)),
            (mix, load(b_own) + load(b_cross, 1), load(b_mate) + load(b_cross, 0)),
            (high, load(c_same), load(c_cross)),
        )
        for band in range(2):
            total = -sum(jnp.where(flag == band, same, other) for flag, same, other in terms)
            out[band, 2 * p] = total[: 2 * THIRD, :NG]
            tail = [total[THIRD * g : THIRD * g + THIRD, NG:] for g in range(3)]
            out[band, 2 * p + 1, :THIRD] = total[2 * THIRD :, :NG]
            out[band, 2 * p + 1, THIRD:] = jnp.concatenate(tail, axis=1)


def unpack(place, *parts):
    steps = 3
    per = PAIRS // steps
    specs = {3: one_slab(per), 4: two_slabs(per)}
    return pl.pallas_call(
        unpack_kernel,
        grid=(steps,),
        in_specs=[pl.BlockSpec(memory_space=pltpu.SMEM)] + [specs[v.ndim] for v in parts],
        out_specs=pl.BlockSpec((2, 2 * per, NG, NG), lambda i: (0, i, 0, 0)),
        out_shape=jax.ShapeDtypeStruct((2, 2 * PAIRS, NG, NG), F32),
        compiler_params=pltpu.CompilerParams(vmem_limit_bytes=SMALL_VMEM),
        name="unpack",
    )(place, *parts)


def transform(left, right, tables, grid_values, lines, emit):
    y_table, y_back, x_table, x_back, z_table, z_back, weights = tables
    flat = lambda v: v.reshape(-1, v.shape[-1])

    for r in range(4):
        held = lines.at[r % 2]

        def forward_z(i, carry, r=r, held=held):
            part = pl.ds(i * BATCH, BATCH)
            density = left[r][part] * right[r][part]
            sums = [
                dot(flat(density[:, THIRD * g : THIRD * g + THIRD]), z_table[g]) for g in range(3)
            ]
            tail = sums[0][:, LANES:] + sums[1][:, LANES:] + sums[2][:, LANES:]
            keep = lambda v: v.astype(BF).reshape(BATCH, THIRD, LANES)
            held[part, :THIRD, :LANES] = keep(sums[0][:, :LANES])
            held[part, THIRD:, :LANES] = keep(sums[1][:, :LANES])
            held[part, :THIRD, LANES:] = keep(sums[2][:, :LANES])
            held[part, THIRD:, LANES:] = keep(tail)
            return carry

        def forward_y(p, carry, r=r, held=held):
            values = dot(y_table[...], held[p])
            x = r * 2 * PAIRS + 2 * p
            grid_values[pl.ds(x, NG, stride=NG), :] = values[:, :LANES]
            grid_values[pl.ds(x + 1, NG, stride=NG), :] = values[:, LANES:]
            return carry

        lax.fori_loop(0, PAIRS // BATCH, forward_z, 0, unroll=True)
        lax.fori_loop(0, PAIRS, forward_y, 0, unroll=True)

    def middle(q, carry):
        upper = pl.ds(pl.multiple_of(q * 2 * NG, 2 * NG), NG)
        lower = pl.ds(pl.multiple_of(q * 2 * NG + NG, NG), NG)
        block = jnp.concatenate([grid_values[upper, :], grid_values[lower, :]], axis=1).astype(BF)
        scaled = weights[pl.ds(pl.multiple_of(q * NG, NG), NG), :] * dot(x_table[...], block)
        back = dot(x_back[...], scaled.astype(BF))
        grid_values[upper, :] = back[:, :LANES]
        grid_values[lower, :] = back[:, LANES:]
        return carry

    lax.fori_loop(0, NG // 2, middle, 0, unroll=16)

    for r in range(4):
        held = lines.at[r % 2]

        def inverse_y(p, carry, r=r, held=held):
            x = r * 2 * PAIRS + 2 * p
            one = grid_values[pl.ds(x, NG, stride=NG), :]
            two = grid_values[pl.ds(x + 1, NG, stride=NG), :]
            held[p] = dot(y_back[...], jnp.concatenate([one, two], axis=1).astype(BF)).astype(BF)
            return carry

        def inverse_z(i, carry, r=r, held=held):
            part = pl.ds(i * BATCH, BATCH)
            last = flat(held[part, THIRD:, LANES:])
            heads = (
                held[part, :THIRD, :LANES],
                held[part, THIRD:, :LANES],
                held[part, :THIRD, LANES:],
            )
            for g in range(3):
                values = dot(jnp.concatenate([flat(heads[g]), last], axis=1), z_back[g])
                at = (part, slice(THIRD * g, THIRD * g + THIRD))
                emit(r, at, values.astype(BF).reshape(BATCH, THIRD, LANES))
            return carry

        lax.fori_loop(0, PAIRS, inverse_y, 0, unroll=True)
        lax.fori_loop(0, PAIRS // BATCH, inverse_z, 0, unroll=True)


def slabs_of(refs, count):
    parts = [ref if len(ref.shape) == 3 else ref.at[0] for ref in refs[: 4 * count]]
    return [parts[4 * n : 4 * n + 4] for n in range(count)]


def first_kernel(*refs):
    a, b = slabs_of(refs[7:], 2)
    field_ab = refs[15:19]

    def emit(r, at, potential):
        field_ab[r][at] = potential

    transform(a, b, refs[:7], *refs[19:], emit)


def second_kernel(*refs):
    a, b, c = slabs_of(refs[7:], 3)
    field_ab, field_bc, out_b = refs[19:23], refs[23:27], refs[27:31]

    def emit(r, at, potential):
        field_bc[r][at] = potential
        total = field_ab[r][at].astype(F32) * a[r][at].astype(F32)
        out_b[r][at] = (total + potential.astype(F32) * c[r][at].astype(F32)).astype(BF)

    transform(b, c, refs[:7], *refs[31:], emit)


def third_kernel(*refs):
    a, b, c = slabs_of(refs[7:], 3)
    field_ab, field_bc, out_a, out_c = refs[19:23], refs[23:27], refs[27:31], refs[31:35]

    def emit(r, at, potential):
        field = potential.astype(F32)
        one, two, three = (v[r][at].astype(F32) for v in (a, b, c))
        out_a[r][at] = (field_ab[r][at].astype(F32) * two + field * three).astype(BF)
        out_c[r][at] = (field_bc[r][at].astype(F32) * two + field * one).astype(BF)

    transform(a, c, refs[:7], *refs[35:], emit)


def call_transform(kernel, name, tables, slabs, outs, flops=1 << 20):
    return pl.pallas_call(
        kernel,
        in_specs=[pl.BlockSpec(memory_space=pltpu.VMEM)] * (len(tables) + len(slabs)),
        out_specs=[pl.BlockSpec(memory_space=pltpu.VMEM)] * outs,
        out_shape=[shape_of(1)] * outs,
        scratch_shapes=[
            pltpu.VMEM((NG * NG, LANES), F32),
            pltpu.VMEM((2, PAIRS, NG, 2 * LANES), BF),
        ],
        compiler_params=pltpu.CompilerParams(vmem_limit_bytes=LARGE_VMEM),
        cost_estimate=pl.CostEstimate(
            flops=flops, bytes_accessed=1 << 14, transcendentals=0
        ),
        name=name,
    )(*tables, *slabs)


def sum_kernel(kept_same, kept_cross, other_same, other_cross, same, cross):
    same[...] = (kept_same[...].astype(F32) + other_same[...].astype(F32)).astype(BF)
    cross[...] = (kept_cross[...].astype(F32) + other_cross[...].astype(F32)).astype(BF)


def add_halves(*slabs):
    return pl.pallas_call(
        sum_kernel,
        out_shape=[shape_of(1)] * 2,
        compiler_params=pltpu.CompilerParams(vmem_limit_bytes=SMALL_VMEM),
        name="add_halves",
    )(*slabs)


def passed(value, blocks, by, length):
    pairs = [
        (4 * k + s, 4 * ((k + by) % length) + (s ^ blocks)) for k in range(length) for s in range(4)
    ]
    return lax.ppermute(value, AXES, pairs)


def per_device(bands):
    length = lax.axis_size("band")
    me = lax.axis_index("grid")
    place = jnp.stack([me // 2, me % 2]).astype(jnp.int32)
    send = functools.partial(passed, length=length)

    table = dft_table(NG)
    orders = [np.concatenate([np.arange(24) + 24 * (r ^ s) for r in range(4)]) for s in range(4)]
    both = np.stack([np.stack([table[:, order], table[:, order].T]) for order in orders])
    x_tables = lax.dynamic_index_in_dim(jnp.asarray(both, BF), me, 0, keepdims=False)

    for_a, for_b, b_keep, b_give, c_same, c_other = pack(place, bands)
    moved = (
        send(c_same, 0, 2),
        send(c_other, 2, 2),
        send(for_b, 2, 0),
        send(for_a, 0, -1),
        send(for_a, 2, -1),
    )
    moved, x_tables = lax.optimization_barrier((moved, x_tables))
    c_same, c_cross, b_cross, a_same, a_cross = moved
    to_mate = lambda value: send(value, 1, 0)
    b = [b_keep, to_mate(b_give), b_cross, to_mate(b_cross[1])]
    a = [a_same, to_mate(a_same[1]), a_cross, to_mate(a_cross[1])]

    y_table, y_back = jnp.asarray(table, BF), jnp.asarray(table.T, BF)
    tables = (y_table, y_back, x_tables[0], x_tables[1], *z_tables(), multiplier())
    field_ab = call_transform(first_kernel, "pair_ab", tables, [*a, *b], 4, FIRST)
    c = [c_same, to_mate(c_same), c_cross, to_mate(c_cross)]
    outs = call_transform(second_kernel, "pair_bc", tables, [*a, *b, *c, *field_ab], 8)
    field_bc, out_b = outs[:4], outs[4:]
    b_mate = to_mate(out_b[1])
    b_cross = jnp.stack([out_b[2], to_mate(out_b[3])])
    b_cross, field_bc = lax.optimization_barrier((b_cross, field_bc))
    b_cross = send(b_cross, 2, 0)
    outs = call_transform(
        third_kernel, "pair_ac", tables, [*a, *b, *c, *field_ab, *field_bc], 8
    )
    out_a, out_c = outs[:4], outs[4:]
    c_same, c_cross = add_halves(out_c[0], out_c[2], to_mate(out_c[1]), to_mate(out_c[3]))
    a_same = jnp.stack([out_a[0], to_mate(out_a[1])])
    a_cross = jnp.stack([out_a[2], to_mate(out_a[3])])
    b_mate, b_cross, a_same, a_cross, c_same, c_cross = lax.optimization_barrier(
        (b_mate, b_cross, a_same, a_cross, c_same, c_cross)
    )
    a_same, a_cross = send(a_same, 0, 1), send(a_cross, 2, 1)
    c_same, c_cross = send(c_same, 0, -2), send(c_cross, 2, -2)
    return unpack(place, a_same, a_cross, b_cross, out_b[0], b_mate, c_same, c_cross)


def solution(mesh):
    spec = P("band", "grid", None, None)
    return jax.shard_map(
        per_device, mesh=mesh, in_specs=(spec,), out_specs=spec, check_vma=False
    )
```

```python
import functools

import jax
import jax.numpy as jnp
import numpy as np
from jax import lax
from jax.experimental import pallas as pl
from jax.experimental.pallas import tpu as pltpu
from jax.sharding import PartitionSpec as P


NG = 96
PAIRS = 12
ROWS = 144
THIRD = 48
LANES = 128
SLAB = PAIRS * ROWS
KERNEL_SCALE = 16.0
SCREEN_SQ = 0.05
AXES = ("band", "grid")
BF = jnp.bfloat16
F32 = jnp.float32
BATCH = 6
FIRST = 12 * 100 * NG**4
SMALL_VMEM = 24 << 20
LARGE_VMEM = 30 << 20


def dft_table(length):
    half = length // 2
    rows = np.arange(length)
    freq = np.where(rows <= half, rows, rows - half)
    phase = 2.0 * np.pi * np.outer(freq, rows) / length
    return np.where((rows <= half)[:, None], np.cos(phase), np.sin(phase))


def z_tables():
    table = dft_table(NG)
    forward = np.zeros((3, LANES, 2 * LANES))
    inverse = np.zeros((3, 2 * LANES, LANES))
    for g in range(3):
        part = table[:, 32 * g : 32 * g + 32]
        forward[g, :NG, :NG] = table.T
        forward[g, NG:, LANES : LANES + NG] = part.T
        inverse[g, :NG, :NG] = table
        inverse[g, LANES : LANES + NG, NG:] = part
    return jnp.asarray(forward, BF), jnp.asarray(inverse, BF)


def frequency_weights(rows):
    freq = jnp.where(rows <= NG // 2, rows, rows - NG // 2).astype(F32)
    weight = jnp.where((rows == 0) | (rows == NG // 2), 1.0, 2.0) / NG
    return freq * freq, jnp.where(rows < NG, weight, 0.0)


def multiplier_kernel(out):
    dims = (NG, 2 * LANES)
    lane = lax.broadcasted_iota(jnp.int32, dims, 1)
    square_a, weight_a = frequency_weights(lax.broadcasted_iota(jnp.int32, dims, 0))
    square_c, weight_c = frequency_weights(lane % LANES)
    square = square_a + square_c + SCREEN_SQ
    scale = KERNEL_SCALE * weight_a * weight_c
    for q in range(NG // 2):
        even, odd = (frequency_weights(jnp.int32(2 * q + n)) for n in range(2))
        square_b, weight_b = (jnp.where(lane < LANES, *pair) for pair in zip(even, odd))
        out[q * NG : q * NG + NG, :] = scale * weight_b / (square + square_b)


def multiplier():
    return pl.pallas_call(
        multiplier_kernel,
        out_shape=jax.ShapeDtypeStruct((NG // 2 * NG, 2 * LANES), F32),
        compiler_params=pltpu.CompilerParams(vmem_limit_bytes=SMALL_VMEM),
        name="multiplier",
    )()


def dot(left, right):
    return jnp.dot(left, right, preferred_element_type=F32)


def pack_kernel(place, bands, for_a, for_b, b_keep, b_give, c_same, c_other):
    high, core = place[0], place[1]
    mix = high ^ core
    for p in range(bands.shape[1] // 2):
        packed = []
        for band in range(2):
            first, second = bands[band, 2 * p], bands[band, 2 * p + 1]
            heads = (first[:THIRD], first[THIRD:], second[:THIRD])
            rows = [
                jnp.concatenate([heads[g], second[THIRD:, 32 * g : 32 * g + 32]], axis=1)
                for g in range(3)
            ]
            packed.append(jnp.concatenate(rows, axis=0))
        pick = lambda flag: jnp.where(flag == 0, packed[0], packed[1]).astype(BF)
        for_a[0, p], for_a[1, p] = pick(core), pick(1 - core)
        mix_same, mix_other = pick(mix), pick(1 - mix)
        for_b[0, p], for_b[1, p] = mix_other, mix_same
        b_keep[p], b_give[p] = mix_same, mix_other
        c_same[p], c_other[p] = pick(high), pick(1 - high)


def one_slab(per):
    return pl.BlockSpec((per, ROWS, LANES), lambda i: (i, 0, 0))


def two_slabs(per):
    return pl.BlockSpec((2, per, ROWS, LANES), lambda i: (0, i, 0, 0))


def shape_of(count):
    dims = (PAIRS, ROWS, LANES)
    return jax.ShapeDtypeStruct(dims if count == 1 else (count, *dims), BF)


def pack(place, bands):
    steps = 3
    per = PAIRS // steps
    return pl.pallas_call(
        pack_kernel,
        grid=(steps,),
        in_specs=[
            pl.BlockSpec(memory_space=pltpu.SMEM),
            pl.BlockSpec((2, 2 * per, NG, NG), lambda i: (0, i, 0, 0)),
        ],
        out_specs=[two_slabs(per)] * 2 + [one_slab(per)] * 4,
        out_shape=[shape_of(2)] * 2 + [shape_of(1)] * 4,
        compiler_params=pltpu.CompilerParams(vmem_limit_bytes=SMALL_VMEM),
        name="pack",
    )(place, bands)


def unpack_kernel(place, a_same, a_cross, b_cross, b_own, b_mate, c_same, c_cross, out):
    high, core = place[0], place[1]
    mix = high ^ core
    for p in range(out.shape[1] // 2):
        load = lambda ref, *at: ref[(*at, p)].astype(F32)
        terms = (
            (core, load(a_same, 0) + load(a_cross, 0), load(a_same, 1) + load(a_cross, 1)),
            (mix, load(b_own) + load(b_cross, 1), load(b_mate) + load(b_cross, 0)),
            (high, load(c_same), load(c_cross)),
        )
        for band in range(2):
            total = -sum(jnp.where(flag == band, same, other) for flag, same, other in terms)
            out[band, 2 * p] = total[: 2 * THIRD, :NG]
            tail = [total[THIRD * g : THIRD * g + THIRD, NG:] for g in range(3)]
            out[band, 2 * p + 1, :THIRD] = total[2 * THIRD :, :NG]
            out[band, 2 * p + 1, THIRD:] = jnp.concatenate(tail, axis=1)


def unpack(place, *parts):
    steps = 3
    per = PAIRS // steps
    specs = {3: one_slab(per), 4: two_slabs(per)}
    return pl.pallas_call(
        unpack_kernel,
        grid=(steps,),
        in_specs=[pl.BlockSpec(memory_space=pltpu.SMEM)] + [specs[v.ndim] for v in parts],
        out_specs=pl.BlockSpec((2, 2 * per, NG, NG), lambda i: (0, i, 0, 0)),
        out_shape=jax.ShapeDtypeStruct((2, 2 * PAIRS, NG, NG), F32),
        compiler_params=pltpu.CompilerParams(vmem_limit_bytes=SMALL_VMEM),
        name="unpack",
    )(place, *parts)


def transform(left, right, tables, grid_values, lines, emit):
    y_table, y_back, x_table, x_back, z_table, z_back, weights = tables
    flat = lambda v: v.reshape(-1, v.shape[-1])

    for r in range(4):
        held = lines.at[r % 2]

        def forward_z(i, carry, r=r, held=held):
            part = pl.ds(i * BATCH, BATCH)
            density = left[r][part] * right[r][part]
            sums = [
                dot(flat(density[:, THIRD * g : THIRD * g + THIRD]), z_table[g]) for g in range(3)
            ]
            tail = sums[0][:, LANES:] + sums[1][:, LANES:] + sums[2][:, LANES:]
            keep = lambda v: v.astype(BF).reshape(BATCH, THIRD, LANES)
            held[part, :THIRD, :LANES] = keep(sums[0][:, :LANES])
            held[part, THIRD:, :LANES] = keep(sums[1][:, :LANES])
            held[part, :THIRD, LANES:] = keep(sums[2][:, :LANES])
            held[part, THIRD:, LANES:] = keep(tail)
            return carry

        def forward_y(p, carry, r=r, held=held):
            values = dot(y_table[...], held[p])
            x = r * 2 * PAIRS + 2 * p
            grid_values[pl.ds(x, NG, stride=NG), :] = values[:, :LANES]
            grid_values[pl.ds(x + 1, NG, stride=NG), :] = values[:, LANES:]
            return carry

        lax.fori_loop(0, PAIRS // BATCH, forward_z, 0, unroll=True)
        lax.fori_loop(0, PAIRS, forward_y, 0, unroll=True)

    def middle(q, carry):
        upper = pl.ds(pl.multiple_of(q * 2 * NG, 2 * NG), NG)
        lower = pl.ds(pl.multiple_of(q * 2 * NG + NG, NG), NG)
        block = jnp.concatenate([grid_values[upper, :], grid_values[lower, :]], axis=1).astype(BF)
        scaled = weights[pl.ds(pl.multiple_of(q * NG, NG), NG), :] * dot(x_table[...], block)
        back = dot(x_back[...], scaled.astype(BF))
        grid_values[upper, :] = back[:, :LANES]
        grid_values[lower, :] = back[:, LANES:]
        return carry

    lax.fori_loop(0, NG // 2, middle, 0, unroll=16)

    for r in range(4):
        held = lines.at[r % 2]

        def inverse_y(p, carry, r=r, held=held):
            x = r * 2 * PAIRS + 2 * p
            one = grid_values[pl.ds(x, NG, stride=NG), :]
            two = grid_values[pl.ds(x + 1, NG, stride=NG), :]
            held[p] = dot(y_back[...], jnp.concatenate([one, two], axis=1).astype(BF)).astype(BF)
            return carry

        def inverse_z(i, carry, r=r, held=held):
            part = pl.ds(i * BATCH, BATCH)
            last = flat(held[part, THIRD:, LANES:])
            heads = (
                held[part, :THIRD, :LANES],
                held[part, THIRD:, :LANES],
                held[part, :THIRD, LANES:],
            )
            for g in range(3):
                values = dot(jnp.concatenate([flat(heads[g]), last], axis=1), z_back[g])
                at = (part, slice(THIRD * g, THIRD * g + THIRD))
                emit(r, at, values.astype(BF).reshape(BATCH, THIRD, LANES))
            return carry

        lax.fori_loop(0, PAIRS, inverse_y, 0, unroll=True)
        lax.fori_loop(0, PAIRS // BATCH, inverse_z, 0, unroll=True)


def slabs_of(refs, count):
    parts = [ref if len(ref.shape) == 3 else ref.at[0] for ref in refs[: 4 * count]]
    return [parts[4 * n : 4 * n + 4] for n in range(count)]


def first_kernel(*refs):
    a, b = slabs_of(refs[7:], 2)
    field_ab = refs[15:19]

    def emit(r, at, potential):
        field_ab[r][at] = potential

    transform(a, b, refs[:7], *refs[19:], emit)


def second_kernel(*refs):
    a, b, c = slabs_of(refs[7:], 3)
    field_ab, field_bc, out_b = refs[19:23], refs[23:27], refs[27:31]

    def emit(r, at, potential):
        field_bc[r][at] = potential
        total = field_ab[r][at].astype(F32) * a[r][at].astype(F32)
        out_b[r][at] = (total + potential.astype(F32) * c[r][at].astype(F32)).astype(BF)

    transform(b, c, refs[:7], *refs[31:], emit)


def third_kernel(*refs):
    a, b, c = slabs_of(refs[7:], 3)
    field_ab, field_bc, out_a, out_c = refs[19:23], refs[23:27], refs[27:31], refs[31:35]

    def emit(r, at, potential):
        field = potential.astype(F32)
        one, two, three = (v[r][at].astype(F32) for v in (a, b, c))
        out_a[r][at] = (field_ab[r][at].astype(F32) * two + field * three).astype(BF)
        out_c[r][at] = (field_bc[r][at].astype(F32) * two + field * one).astype(BF)

    transform(a, c, refs[:7], *refs[35:], emit)


def call_transform(kernel, name, tables, slabs, outs, flops=1 << 20):
    return pl.pallas_call(
        kernel,
        in_specs=[pl.BlockSpec(memory_space=pltpu.VMEM)] * (len(tables) + len(slabs)),
        out_specs=[pl.BlockSpec(memory_space=pltpu.VMEM)] * outs,
        out_shape=[shape_of(1)] * outs,
        scratch_shapes=[
            pltpu.VMEM((NG * NG, LANES), F32),
            pltpu.VMEM((2, PAIRS, NG, 2 * LANES), BF),
        ],
        compiler_params=pltpu.CompilerParams(vmem_limit_bytes=LARGE_VMEM),
        cost_estimate=pl.CostEstimate(
            flops=flops, bytes_accessed=1 << 14, transcendentals=0
        ),
        name=name,
    )(*tables, *slabs)


def sum_kernel(kept_same, kept_cross, other_same, other_cross, same, cross):
    same[...] = (kept_same[...].astype(F32) + other_same[...].astype(F32)).astype(BF)
    cross[...] = (kept_cross[...].astype(F32) + other_cross[...].astype(F32)).astype(BF)


def add_halves(*slabs):
    return pl.pallas_call(
        sum_kernel,
        out_shape=[shape_of(1)] * 2,
        compiler_params=pltpu.CompilerParams(vmem_limit_bytes=SMALL_VMEM),
        name="add_halves",
    )(*slabs)


def passed(value, blocks, by, length):
    pairs = [
        (4 * k + s, 4 * ((k + by) % length) + (s ^ blocks)) for k in range(length) for s in range(4)
    ]
    return lax.ppermute(value, AXES, pairs)


def per_device(bands):
    length = lax.axis_size("band")
    me = lax.axis_index("grid")
    place = jnp.stack([me // 2, me % 2]).astype(jnp.int32)
    send = functools.partial(passed, length=length)

    table = dft_table(NG)
    orders = [np.concatenate([np.arange(24) + 24 * (r ^ s) for r in range(4)]) for s in range(4)]
    both = np.stack([np.stack([table[:, order], table[:, order].T]) for order in orders])
    x_tables = lax.dynamic_index_in_dim(jnp.asarray(both, BF), me, 0, keepdims=False)

    for_a, for_b, b_keep, b_give, c_same, c_other = pack(place, bands)
    moved = (
        send(c_same, 0, 2),
        send(c_other, 2, 2),
        send(for_b, 2, 0),
        send(for_a, 0, -1),
        send(for_a, 2, -1),
    )
    moved, x_tables = lax.optimization_barrier((moved, x_tables))
    c_same, c_cross, b_cross, a_same, a_cross = moved
    to_mate = lambda value: send(value, 1, 0)
    b = [b_keep, to_mate(b_give), b_cross, to_mate(b_cross[1])]
    a = [a_same, to_mate(a_same[1]), a_cross, to_mate(a_cross[1])]

    y_table, y_back = jnp.asarray(table, BF), jnp.asarray(table.T, BF)
    tables = (y_table, y_back, x_tables[0], x_tables[1], *z_tables(), multiplier())
    field_ab = call_transform(first_kernel, "pair_ab", tables, [*a, *b], 4, FIRST)
    c = [c_same, to_mate(c_same), c_cross, to_mate(c_cross)]
    outs = call_transform(second_kernel, "pair_bc", tables, [*a, *b, *c, *field_ab], 8)
    field_bc, out_b = outs[:4], outs[4:]
    b_mate = to_mate(out_b[1])
    b_cross = jnp.stack([out_b[2], to_mate(out_b[3])])
    b_mate, b_cross, field_bc = lax.optimization_barrier((b_mate, b_cross, field_bc))
    b_cross = send(b_cross, 2, 0)
    outs = call_transform(
        third_kernel, "pair_ac", tables, [*a, *b, *c, *field_ab, *field_bc], 8
    )
    out_a, out_c = outs[:4], outs[4:]
    c_same, c_cross = add_halves(out_c[0], out_c[2], to_mate(out_c[1]), to_mate(out_c[3]))
    a_same = jnp.stack([out_a[0], to_mate(out_a[1])])
    a_cross = jnp.stack([out_a[2], to_mate(out_a[3])])
    b_cross, a_same, a_cross, c_same, c_cross = lax.optimization_barrier(
        (b_cross, a_same, a_cross, c_same, c_cross)
    )
    a_same, a_cross = send(a_same, 0, 1), send(a_cross, 2, 1)
    c_same, c_cross = send(c_same, 0, -2), send(c_cross, 2, -2)
    return unpack(place, a_same, a_cross, b_cross, out_b[0], b_mate, c_same, c_cross)


def solution(mesh):
    spec = P("band", "grid", None, None)
    return jax.shard_map(
        per_device, mesh=mesh, in_specs=(spec,), out_specs=spec, check_vma=False
    )
```

```python
import functools

import jax
import jax.numpy as jnp
import numpy as np
from jax import lax
from jax.experimental import pallas as pl
from jax.experimental.pallas import tpu as pltpu
from jax.sharding import PartitionSpec as P


NG = 96
PAIRS = 12
ROWS = 144
THIRD = 48
LANES = 128
SLAB = PAIRS * ROWS
KERNEL_SCALE = 16.0
SCREEN_SQ = 0.05
AXES = ("band", "grid")
BF = jnp.bfloat16
F32 = jnp.float32
BATCH = 6
STEPS = 4
SMALL_VMEM = 24 << 20
LARGE_VMEM = 30 << 20


def dft_table(length):
    half = length // 2
    rows = np.arange(length)
    freq = np.where(rows <= half, rows, rows - half)
    phase = 2.0 * np.pi * np.outer(freq, rows) / length
    return np.where((rows <= half)[:, None], np.cos(phase), np.sin(phase))


def z_tables():
    table = dft_table(NG)
    forward = np.zeros((3, LANES, 2 * LANES))
    inverse = np.zeros((3, 2 * LANES, LANES))
    for g in range(3):
        part = table[:, 32 * g : 32 * g + 32]
        forward[g, :NG, :NG] = table.T
        forward[g, NG:, LANES : LANES + NG] = part.T
        inverse[g, :NG, :NG] = table
        inverse[g, LANES : LANES + NG, NG:] = part
    return jnp.asarray(forward, BF), jnp.asarray(inverse, BF)


def frequency_weights(rows):
    freq = jnp.where(rows <= NG // 2, rows, rows - NG // 2).astype(F32)
    weight = jnp.where((rows == 0) | (rows == NG // 2), 1.0, 2.0) / NG
    return freq * freq, jnp.where(rows < NG, weight, 0.0)


def multiplier_kernel(out):
    dims = (NG, 2 * LANES)
    lane = lax.broadcasted_iota(jnp.int32, dims, 1)
    square_a, weight_a = frequency_weights(lax.broadcasted_iota(jnp.int32, dims, 0))
    square_c, weight_c = frequency_weights(lane % LANES)
    square = square_a + square_c + SCREEN_SQ
    scale = KERNEL_SCALE * weight_a * weight_c
    for q in range(NG // 2):
        even, odd = (frequency_weights(jnp.int32(2 * q + n)) for n in range(2))
        square_b, weight_b = (jnp.where(lane < LANES, *pair) for pair in zip(even, odd))
        out[q * NG : q * NG + NG, :] = scale * weight_b / (square + square_b)


def multiplier():
    return pl.pallas_call(
        multiplier_kernel,
        out_shape=jax.ShapeDtypeStruct((NG // 2 * NG, 2 * LANES), F32),
        compiler_params=pltpu.CompilerParams(vmem_limit_bytes=SMALL_VMEM),
        name="multiplier",
    )()


def dot(left, right):
    return jnp.dot(left, right, preferred_element_type=F32)


def pack_kernel(
    place, bands, for_a, for_b, b_keep, b_give, c_same, c_other, held, arrived
):
    high, core = place[0], place[1]
    mix = high ^ core
    per = 2 * PAIRS // STEPS
    copies = []
    for step in range(STEPS):
        planes = pl.ds(step * per, per)
        copies.append(
            pltpu.make_async_copy(bands.at[:, planes], held.at[:, planes], arrived.at[step])
        )
        copies[-1].start()
    for p in range(PAIRS):
        if 2 * p % per == 0:
            copies[2 * p // per].wait()
        packed = []
        for band in range(2):
            first, second = held[band, 2 * p], held[band, 2 * p + 1]
            heads = (first[:THIRD], first[THIRD:], second[:THIRD])
            rows = [
                jnp.concatenate([heads[g], second[THIRD:, 32 * g : 32 * g + 32]], axis=1)
                for g in range(3)
            ]
            packed.append(jnp.concatenate(rows, axis=0))
        pick = lambda flag: jnp.where(flag == 0, packed[0], packed[1]).astype(BF)
        for_a[0, p], for_a[1, p] = pick(core), pick(1 - core)
        mix_same, mix_other = pick(mix), pick(1 - mix)
        for_b[0, p], for_b[1, p] = mix_other, mix_same
        b_keep[p], b_give[p] = mix_same, mix_other
        c_same[p], c_other[p] = pick(high), pick(1 - high)


def shape_of(count):
    dims = (PAIRS, ROWS, LANES)
    return jax.ShapeDtypeStruct(dims if count == 1 else (count, *dims), BF)


def pack(place, bands):
    return pl.pallas_call(
        pack_kernel,
        in_specs=[
            pl.BlockSpec(memory_space=pltpu.SMEM),
            pl.BlockSpec(memory_space=pltpu.HBM),
        ],
        out_specs=[pl.BlockSpec(memory_space=pltpu.VMEM)] * 6,
        out_shape=[shape_of(2)] * 2 + [shape_of(1)] * 4,
        scratch_shapes=[
            pltpu.VMEM((2, 2 * PAIRS, NG, NG), F32),
            pltpu.SemaphoreType.DMA((STEPS,)),
        ],
        compiler_params=pltpu.CompilerParams(vmem_limit_bytes=SMALL_VMEM),
        name="pack",
    )(place, bands)


def unpack_kernel(place, a_same, a_cross, b_cross, b_own, b_mate, c_same, c_cross, out):
    high, core = place[0], place[1]
    mix = high ^ core
    per = out.shape[1] // 2
    start = pl.program_id(0) * per
    for p in range(per):
        load = lambda ref, *at: ref[(*at, start + p)].astype(F32)
        terms = (
            (core, load(a_same, 0) + load(a_cross, 0), load(a_same, 1) + load(a_cross, 1)),
            (mix, load(b_own) + load(b_cross, 1), load(b_mate, 0) + load(b_cross, 0)),
            (high, load(c_same), load(c_cross)),
        )
        for band in range(2):
            total = -sum(jnp.where(flag == band, same, other) for flag, same, other in terms)
            out[band, 2 * p] = total[: 2 * THIRD, :NG]
            tail = [total[THIRD * g : THIRD * g + THIRD, NG:] for g in range(3)]
            out[band, 2 * p + 1, :THIRD] = total[2 * THIRD :, :NG]
            out[band, 2 * p + 1, THIRD:] = jnp.concatenate(tail, axis=1)


def unpack(place, *parts):
    per = PAIRS // STEPS
    return pl.pallas_call(
        unpack_kernel,
        grid=(STEPS,),
        in_specs=[pl.BlockSpec(memory_space=pltpu.SMEM)]
        + [pl.BlockSpec(memory_space=pltpu.VMEM)] * len(parts),
        out_specs=pl.BlockSpec((2, 2 * per, NG, NG), lambda i: (0, i, 0, 0)),
        out_shape=jax.ShapeDtypeStruct((2, 2 * PAIRS, NG, NG), F32),
        compiler_params=pltpu.CompilerParams(vmem_limit_bytes=SMALL_VMEM),
        name="unpack",
    )(place, *parts)


def transform(left, right, tables, grid_values, lines, emit):
    y_table, y_back, x_table, x_back, z_table, z_back, weights = tables
    flat = lambda v: v.reshape(-1, v.shape[-1])

    for r in range(4):
        held = lines.at[r % 2]

        def forward_z(i, carry, r=r, held=held):
            part = pl.ds(i * BATCH, BATCH)
            density = left[r][part] * right[r][part]
            sums = [
                dot(flat(density[:, THIRD * g : THIRD * g + THIRD]), z_table[g]) for g in range(3)
            ]
            tail = sums[0][:, LANES:] + sums[1][:, LANES:] + sums[2][:, LANES:]
            keep = lambda v: v.astype(BF).reshape(BATCH, THIRD, LANES)
            held[part, :THIRD, :LANES] = keep(sums[0][:, :LANES])
            held[part, THIRD:, :LANES] = keep(sums[1][:, :LANES])
            held[part, :THIRD, LANES:] = keep(sums[2][:, :LANES])
            held[part, THIRD:, LANES:] = keep(tail)
            return carry

        def forward_y(p, carry, r=r, held=held):
            values = dot(y_table[...], held[p])
            x = r * 2 * PAIRS + 2 * p
            grid_values[pl.ds(x, NG, stride=NG), :] = values[:, :LANES]
            grid_values[pl.ds(x + 1, NG, stride=NG), :] = values[:, LANES:]
            return carry

        lax.fori_loop(0, PAIRS // BATCH, forward_z, 0, unroll=True)
        lax.fori_loop(0, PAIRS, forward_y, 0, unroll=True)

    def middle(q, carry):
        upper = pl.ds(pl.multiple_of(q * 2 * NG, 2 * NG), NG)
        lower = pl.ds(pl.multiple_of(q * 2 * NG + NG, NG), NG)
        block = jnp.concatenate([grid_values[upper, :], grid_values[lower, :]], axis=1).astype(BF)
        scaled = weights[pl.ds(pl.multiple_of(q * NG, NG), NG), :] * dot(x_table[...], block)
        back = dot(x_back[...], scaled.astype(BF))
        grid_values[upper, :] = back[:, :LANES]
        grid_values[lower, :] = back[:, LANES:]
        return carry

    lax.fori_loop(0, NG // 2, middle, 0, unroll=16)

    for r in range(4):
        held = lines.at[r % 2]

        def inverse_y(p, carry, r=r, held=held):
            x = r * 2 * PAIRS + 2 * p
            one = grid_values[pl.ds(x, NG, stride=NG), :]
            two = grid_values[pl.ds(x + 1, NG, stride=NG), :]
            held[p] = dot(y_back[...], jnp.concatenate([one, two], axis=1).astype(BF)).astype(BF)
            return carry

        def inverse_z(i, carry, r=r, held=held):
            part = pl.ds(i * BATCH, BATCH)
            last = flat(held[part, THIRD:, LANES:])
            heads = (
                held[part, :THIRD, :LANES],
                held[part, THIRD:, :LANES],
                held[part, :THIRD, LANES:],
            )
            for g in range(3):
                values = dot(jnp.concatenate([flat(heads[g]), last], axis=1), z_back[g])
                at = (part, slice(THIRD * g, THIRD * g + THIRD))
                emit(r, at, values.astype(BF).reshape(BATCH, THIRD, LANES))
            return carry

        lax.fori_loop(0, PAIRS, inverse_y, 0, unroll=True)
        lax.fori_loop(0, PAIRS // BATCH, inverse_z, 0, unroll=True)


def slabs_of(refs, count):
    parts = [ref if len(ref.shape) == 3 else ref.at[0] for ref in refs[: 4 * count]]
    return [parts[4 * n : 4 * n + 4] for n in range(count)]


def first_kernel(*refs):
    c, b = slabs_of(refs[7:], 2)
    field_cb = refs[15]

    def emit(r, at, potential):
        field_cb[(r, *at)] = potential

    transform(c, b, refs[:7], *refs[16:], emit)


def second_kernel(*refs):
    c, b, a = slabs_of(refs[7:], 3)
    field_cb, field_ca, c_keep, c_give = refs[19:23]
    out = (c_keep.at[0], c_give.at[0], c_keep.at[1], c_give.at[1])

    def emit(r, at, potential):
        field_ca[(r, *at)] = potential
        total = field_cb[(r, *at)].astype(F32) * b[r][at].astype(F32)
        out[r][at] = (total + potential.astype(F32) * a[r][at].astype(F32)).astype(BF)

    transform(c, a, refs[:7], *refs[23:], emit)


def third_kernel(*refs):
    c, b, a = slabs_of(refs[7:], 3)
    field_cb, field_ca, b_own, b_far, b_give, a_own, a_far, a_give = refs[19:27]
    out_b = (b_own, b_give.at[0], b_far, b_give.at[1])
    out_a = (a_own, a_give.at[0], a_far, a_give.at[1])

    def emit(r, at, potential):
        field = potential.astype(F32)
        one, two, three = (v[r][at].astype(F32) for v in (c, b, a))
        out_b[r][at] = (field_cb[(r, *at)].astype(F32) * one + field * three).astype(BF)
        out_a[r][at] = (field_ca[(r, *at)].astype(F32) * one + field * two).astype(BF)

    transform(b, a, refs[:7], *refs[27:], emit)


def call_transform(kernel, name, tables, slabs, outs):
    return pl.pallas_call(
        kernel,
        in_specs=[pl.BlockSpec(memory_space=pltpu.VMEM)] * (len(tables) + len(slabs)),
        out_specs=[pl.BlockSpec(memory_space=pltpu.VMEM)] * len(outs),
        out_shape=[shape_of(count) for count in outs],
        scratch_shapes=[
            pltpu.VMEM((NG * NG, LANES), F32),
            pltpu.VMEM((2, PAIRS, NG, 2 * LANES), BF),
        ],
        compiler_params=pltpu.CompilerParams(vmem_limit_bytes=LARGE_VMEM),
        cost_estimate=pl.CostEstimate(
            flops=1 << 20, bytes_accessed=1 << 16, transcendentals=0
        ),
        name=name,
    )(*tables, *slabs)


def sum_kernel(kept, received, same, cross):
    for n, out in enumerate((same, cross)):
        out[...] = (kept[n].astype(F32) + received[n].astype(F32)).astype(BF)


def add_halves(kept, received):
    return pl.pallas_call(
        sum_kernel,
        out_shape=[shape_of(1)] * 2,
        compiler_params=pltpu.CompilerParams(vmem_limit_bytes=SMALL_VMEM),
        name="add_halves",
    )(kept, received)


def passed(value, blocks, by, length):
    pairs = [
        (4 * k + s, 4 * ((k + by) % length) + (s ^ blocks)) for k in range(length) for s in range(4)
    ]
    return lax.ppermute(value, AXES, pairs)


def per_device(bands):
    length = lax.axis_size("band")
    me = lax.axis_index("grid")
    place = jnp.stack([me // 2, me % 2]).astype(jnp.int32)
    send = functools.partial(passed, length=length)

    table = dft_table(NG)
    orders = [np.concatenate([np.arange(24) + 24 * (r ^ s) for r in range(4)]) for s in range(4)]
    both = np.stack([np.stack([table[:, order], table[:, order].T]) for order in orders])
    x_tables = lax.dynamic_index_in_dim(jnp.asarray(both, BF), me, 0, keepdims=False)

    for_a, for_b, b_keep, b_give, c_same, c_other = pack(place, bands)
    moved = (
        send(c_same, 0, 2),
        send(c_other, 2, 2),
        send(for_b, 2, 0),
        send(for_a, 0, -1),
        send(for_a, 2, -1),
    )
    moved, x_tables = lax.optimization_barrier((moved, x_tables))
    c_same, c_cross, b_cross, a_same, a_cross = moved
    to_mate = lambda value: send(value, 1, 0)
    b = [b_keep, to_mate(b_give), b_cross, to_mate(b_cross[1])]
    a = [a_same, to_mate(a_same[1]), a_cross, to_mate(a_cross[1])]

    c = [c_same, to_mate(c_same), c_cross, to_mate(c_cross)]

    y_table, y_back = jnp.asarray(table, BF), jnp.asarray(table.T, BF)
    tables = (y_table, y_back, x_tables[0], x_tables[1], *z_tables(), multiplier())
    (field_cb,) = call_transform(first_kernel, "pair_cb", tables, [*c, *b], [4])
    field_ca, c_keep, c_give = call_transform(
        second_kernel, "pair_ca", tables, [*c, *b, *a, field_cb], [4, 2, 2]
    )
    sums = add_halves(c_keep, to_mate(c_give))
    c_same, c_cross, field_ca = lax.optimization_barrier((*sums, field_ca))
    c_same, c_cross = send(c_same, 0, -2), send(c_cross, 2, -2)
    b_own, b_far, b_give, a_own, a_far, a_give = call_transform(
        third_kernel, "pair_ba", tables, [*c, *b, *a, field_cb, field_ca], [1, 1, 2, 1, 1, 2]
    )
    a_mate, b_mate = to_mate(a_give), to_mate(b_give)
    a_same = send(jnp.stack([a_own, a_mate[0]]), 0, 1)
    a_cross = send(jnp.stack([a_far, a_mate[1]]), 2, 1)
    b_cross = send(jnp.stack([b_far, b_mate[1]]), 2, 0)
    return unpack(place, a_same, a_cross, b_cross, b_own, b_mate, c_same, c_cross)


def solution(mesh):
    spec = P("band", "grid", None, None)
    return jax.shard_map(
        per_device, mesh=mesh, in_specs=(spec,), out_specs=spec, check_vma=False
    )
```

```python
import functools

import jax
import jax.numpy as jnp
import numpy as np
from jax import lax
from jax.experimental import pallas as pl
from jax.experimental.pallas import tpu as pltpu
from jax.sharding import PartitionSpec as P


NG = 96
PAIRS = 12
ROWS = 144
THIRD = 48
LANES = 128
SLAB = PAIRS * ROWS
KERNEL_SCALE = 16.0
SCREEN_SQ = 0.05
AXES = ("band", "grid")
BF = jnp.bfloat16
F32 = jnp.float32
BATCH = 6
STEPS = 4
SMALL_VMEM = 24 << 20
WHOLE_VMEM = 58 << 20
LARGE_VMEM = 30 << 20


def dft_table(length):
    half = length // 2
    rows = np.arange(length)
    freq = np.where(rows <= half, rows, rows - half)
    phase = 2.0 * np.pi * np.outer(freq, rows) / length
    return np.where((rows <= half)[:, None], np.cos(phase), np.sin(phase))


def z_tables():
    table = dft_table(NG)
    forward = np.zeros((3, LANES, 2 * LANES))
    inverse = np.zeros((3, 2 * LANES, LANES))
    for g in range(3):
        part = table[:, 32 * g : 32 * g + 32]
        forward[g, :NG, :NG] = table.T
        forward[g, NG:, LANES : LANES + NG] = part.T
        inverse[g, :NG, :NG] = table
        inverse[g, LANES : LANES + NG, NG:] = part
    return jnp.asarray(forward, BF), jnp.asarray(inverse, BF)


def frequency_weights(rows):
    freq = jnp.where(rows <= NG // 2, rows, rows - NG // 2).astype(F32)
    weight = jnp.where((rows == 0) | (rows == NG // 2), 1.0, 2.0) / NG
    return freq * freq, jnp.where(rows < NG, weight, 0.0)


def multiplier_kernel(out):
    dims = (NG, 2 * LANES)
    lane = lax.broadcasted_iota(jnp.int32, dims, 1)
    square_a, weight_a = frequency_weights(lax.broadcasted_iota(jnp.int32, dims, 0))
    square_c, weight_c = frequency_weights(lane % LANES)
    square = square_a + square_c + SCREEN_SQ
    scale = KERNEL_SCALE * weight_a * weight_c
    for q in range(NG // 2):
        even, odd = (frequency_weights(jnp.int32(2 * q + n)) for n in range(2))
        square_b, weight_b = (jnp.where(lane < LANES, *pair) for pair in zip(even, odd))
        out[q * NG : q * NG + NG, :] = scale * weight_b / (square + square_b)


def multiplier():
    return pl.pallas_call(
        multiplier_kernel,
        out_shape=jax.ShapeDtypeStruct((NG // 2 * NG, 2 * LANES), F32),
        compiler_params=pltpu.CompilerParams(vmem_limit_bytes=SMALL_VMEM),
        name="multiplier",
    )()


def dot(left, right):
    return jnp.dot(left, right, preferred_element_type=F32)


def pack_kernel(place, bands, for_a, for_b, b_keep, b_give, c_same, c_other):
    high, core = place[0], place[1]
    mix = high ^ core
    for p in range(bands.shape[1] // 2):
        packed = []
        for band in range(2):
            first, second = bands[band, 2 * p], bands[band, 2 * p + 1]
            heads = (first[:THIRD], first[THIRD:], second[:THIRD])
            rows = [
                jnp.concatenate([heads[g], second[THIRD:, 32 * g : 32 * g + 32]], axis=1)
                for g in range(3)
            ]
            packed.append(jnp.concatenate(rows, axis=0))
        pick = lambda flag: jnp.where(flag == 0, packed[0], packed[1]).astype(BF)
        for_a[0, p], for_a[1, p] = pick(core), pick(1 - core)
        mix_same, mix_other = pick(mix), pick(1 - mix)
        for_b[0, p], for_b[1, p] = mix_other, mix_same
        b_keep[p], b_give[p] = mix_same, mix_other
        c_same[p], c_other[p] = pick(high), pick(1 - high)


def one_slab(per):
    return pl.BlockSpec((per, ROWS, LANES), lambda i: (i, 0, 0))


def two_slabs(per):
    return pl.BlockSpec((2, per, ROWS, LANES), lambda i: (0, i, 0, 0))


def shape_of(count):
    dims = (PAIRS, ROWS, LANES)
    return jax.ShapeDtypeStruct(dims if count == 1 else (count, *dims), BF)


def pack(place, bands):
    per = PAIRS // STEPS
    return pl.pallas_call(
        pack_kernel,
        grid=(STEPS,),
        in_specs=[
            pl.BlockSpec(memory_space=pltpu.SMEM),
            pl.BlockSpec((2, 2 * per, NG, NG), lambda i: (0, i, 0, 0)),
        ],
        out_specs=[two_slabs(per)] * 2 + [one_slab(per)] * 4,
        out_shape=[shape_of(2)] * 2 + [shape_of(1)] * 4,
        compiler_params=pltpu.CompilerParams(vmem_limit_bytes=WHOLE_VMEM),
        name="pack",
    )(place, bands)


def unpack_kernel(place, a_same, a_cross, b_cross, b_own, b_mate, c_same, c_cross, out):
    high, core = place[0], place[1]
    mix = high ^ core
    per = out.shape[1] // 2
    start = pl.program_id(0) * per
    for p in range(per):
        load = lambda ref, *at: ref[(*at, start + p)]
        for band in range(2):
            other = core ^ band
            third = jnp.where(mix == band, load(b_own), load(b_mate, 0)).astype(F32)
            fifth = jnp.where(high == band, load(c_same), load(c_cross)).astype(F32)
            total = load(a_same, other).astype(F32) + load(a_cross, other).astype(F32)
            total += third + load(b_cross, 1 - (mix ^ band)).astype(F32)
            total = -(total + fifth)
            out[band, 2 * p] = total[: 2 * THIRD, :NG]
            tail = [total[THIRD * g : THIRD * g + THIRD, NG:] for g in range(3)]
            out[band, 2 * p + 1, :THIRD] = total[2 * THIRD :, :NG]
            out[band, 2 * p + 1, THIRD:] = jnp.concatenate(tail, axis=1)


def unpack(place, *parts):
    per = PAIRS // STEPS
    return pl.pallas_call(
        unpack_kernel,
        grid=(STEPS,),
        in_specs=[pl.BlockSpec(memory_space=pltpu.SMEM)]
        + [pl.BlockSpec(memory_space=pltpu.VMEM)] * len(parts),
        out_specs=pl.BlockSpec((2, 2 * per, NG, NG), lambda i: (0, i, 0, 0)),
        out_shape=jax.ShapeDtypeStruct((2, 2 * PAIRS, NG, NG), F32),
        compiler_params=pltpu.CompilerParams(vmem_limit_bytes=SMALL_VMEM),
        name="unpack",
    )(place, *parts)


def transform(left, right, tables, grid_values, lines, emit):
    y_table, y_back, x_table, x_back, z_table, z_back, weights = tables
    flat = lambda v: v.reshape(-1, v.shape[-1])

    for r in range(4):
        held = lines.at[r % 2]

        def forward_z(i, carry, r=r, held=held):
            part = pl.ds(i * BATCH, BATCH)
            density = left[r][part] * right[r][part]
            sums = [
                dot(flat(density[:, THIRD * g : THIRD * g + THIRD]), z_table[g]) for g in range(3)
            ]
            tail = sums[0][:, LANES:] + sums[1][:, LANES:] + sums[2][:, LANES:]
            keep = lambda v: v.astype(BF).reshape(BATCH, THIRD, LANES)
            held[part, :THIRD, :LANES] = keep(sums[0][:, :LANES])
            held[part, THIRD:, :LANES] = keep(sums[1][:, :LANES])
            held[part, :THIRD, LANES:] = keep(sums[2][:, :LANES])
            held[part, THIRD:, LANES:] = keep(tail)
            return carry

        def forward_y(p, carry, r=r, held=held):
            values = dot(y_table[...], held[p])
            x = r * 2 * PAIRS + 2 * p
            grid_values[pl.ds(x, NG, stride=NG), :] = values[:, :LANES]
            grid_values[pl.ds(x + 1, NG, stride=NG), :] = values[:, LANES:]
            return carry

        lax.fori_loop(0, PAIRS // BATCH, forward_z, 0, unroll=True)
        lax.fori_loop(0, PAIRS, forward_y, 0, unroll=True)

    def middle(q, carry):
        upper = pl.ds(pl.multiple_of(q * 2 * NG, 2 * NG), NG)
        lower = pl.ds(pl.multiple_of(q * 2 * NG + NG, NG), NG)
        block = jnp.concatenate([grid_values[upper, :], grid_values[lower, :]], axis=1).astype(BF)
        scaled = weights[pl.ds(pl.multiple_of(q * NG, NG), NG), :] * dot(x_table[...], block)
        back = dot(x_back[...], scaled.astype(BF))
        grid_values[upper, :] = back[:, :LANES]
        grid_values[lower, :] = back[:, LANES:]
        return carry

    lax.fori_loop(0, NG // 2, middle, 0, unroll=24)

    for r in range(4):
        held = lines.at[r % 2]

        def inverse_y(p, carry, r=r, held=held):
            x = r * 2 * PAIRS + 2 * p
            one = grid_values[pl.ds(x, NG, stride=NG), :]
            two = grid_values[pl.ds(x + 1, NG, stride=NG), :]
            held[p] = dot(y_back[...], jnp.concatenate([one, two], axis=1).astype(BF)).astype(BF)
            return carry

        def inverse_z(i, carry, r=r, held=held):
            part = pl.ds(i * BATCH, BATCH)
            last = flat(held[part, THIRD:, LANES:])
            heads = (
                held[part, :THIRD, :LANES],
                held[part, THIRD:, :LANES],
                held[part, :THIRD, LANES:],
            )
            for g in range(3):
                values = dot(jnp.concatenate([flat(heads[g]), last], axis=1), z_back[g])
                at = (part, slice(THIRD * g, THIRD * g + THIRD))
                emit(r, at, values.astype(BF).reshape(BATCH, THIRD, LANES))
            return carry

        lax.fori_loop(0, PAIRS, inverse_y, 0, unroll=True)
        lax.fori_loop(0, PAIRS // BATCH, inverse_z, 0, unroll=True)


def slabs_of(refs, count):
    parts = [ref if len(ref.shape) == 3 else ref.at[0] for ref in refs[: 4 * count]]
    return [parts[4 * n : 4 * n + 4] for n in range(count)]


def first_kernel(*refs):
    c, b = slabs_of(refs[7:], 2)
    field_cb = refs[15]

    def emit(r, at, potential):
        field_cb[(r, *at)] = potential

    transform(c, b, refs[:7], *refs[16:], emit)


def second_kernel(*refs):
    c, b, a = slabs_of(refs[7:], 3)
    field_cb, field_ca, c_keep, c_give = refs[19:23]
    out = (c_keep.at[0], c_give.at[0], c_keep.at[1], c_give.at[1])

    def emit(r, at, potential):
        field_ca[(r, *at)] = potential
        total = field_cb[(r, *at)].astype(F32) * b[r][at].astype(F32)
        out[r][at] = (total + potential.astype(F32) * a[r][at].astype(F32)).astype(BF)

    transform(c, a, refs[:7], *refs[23:], emit)


def third_kernel(*refs):
    c, b, a = slabs_of(refs[7:], 3)
    field_cb, field_ca, b_own, b_far, b_give, a_own, a_far, a_give = refs[19:27]
    out_b = (b_own, b_give.at[0], b_far, b_give.at[1])
    out_a = (a_own, a_give.at[0], a_far, a_give.at[1])

    def emit(r, at, potential):
        field = potential.astype(F32)
        one, two, three = (v[r][at].astype(F32) for v in (c, b, a))
        out_b[r][at] = (field_cb[(r, *at)].astype(F32) * one + field * three).astype(BF)
        out_a[r][at] = (field_ca[(r, *at)].astype(F32) * one + field * two).astype(BF)

    transform(b, a, refs[:7], *refs[27:], emit)


def call_transform(kernel, name, tables, slabs, outs):
    return pl.pallas_call(
        kernel,
        in_specs=[pl.BlockSpec(memory_space=pltpu.VMEM)] * (len(tables) + len(slabs)),
        out_specs=[pl.BlockSpec(memory_space=pltpu.VMEM)] * len(outs),
        out_shape=[shape_of(count) for count in outs],
        scratch_shapes=[
            pltpu.VMEM((NG * NG, LANES), F32),
            pltpu.VMEM((2, PAIRS, NG, 2 * LANES), BF),
        ],
        compiler_params=pltpu.CompilerParams(vmem_limit_bytes=LARGE_VMEM),
        cost_estimate=pl.CostEstimate(
            flops=1 << 20, bytes_accessed=1 << 16, transcendentals=0
        ),
        name=name,
    )(*tables, *slabs)


def sum_kernel(kept, received, same, cross):
    for n, out in enumerate((same, cross)):
        out[...] = (kept[n].astype(F32) + received[n].astype(F32)).astype(BF)


def add_halves(kept, received):
    return pl.pallas_call(
        sum_kernel,
        out_shape=[shape_of(1)] * 2,
        compiler_params=pltpu.CompilerParams(vmem_limit_bytes=SMALL_VMEM),
        name="add_halves",
    )(kept, received)


def passed(value, blocks, by, length):
    pairs = [
        (4 * k + s, 4 * ((k + by) % length) + (s ^ blocks)) for k in range(length) for s in range(4)
    ]
    return lax.ppermute(value, AXES, pairs)


def per_device(bands):
    length = lax.axis_size("band")
    me = lax.axis_index("grid")
    place = jnp.stack([me // 2, me % 2]).astype(jnp.int32)
    send = functools.partial(passed, length=length)

    table = dft_table(NG)
    orders = [np.concatenate([np.arange(24) + 24 * (r ^ s) for r in range(4)]) for s in range(4)]
    both = np.stack([np.stack([table[:, order], table[:, order].T]) for order in orders])
    x_tables = lax.dynamic_index_in_dim(jnp.asarray(both, BF), me, 0, keepdims=False)

    for_a, for_b, b_keep, b_give, c_same, c_other = pack(place, bands)
    moved = (
        send(c_same, 0, 2),
        send(c_other, 2, 2),
        send(for_b, 2, 0),
        send(for_a, 0, -1),
        send(for_a, 2, -1),
    )
    moved, x_tables = lax.optimization_barrier((moved, x_tables))
    c_same, c_cross, b_cross, a_same, a_cross = moved
    to_mate = lambda value: send(value, 1, 0)
    b = [b_keep, to_mate(b_give), b_cross, to_mate(b_cross[1])]
    a = [a_same, to_mate(a_same[1]), a_cross, to_mate(a_cross[1])]

    c = [c_same, to_mate(c_same), c_cross, to_mate(c_cross)]

    y_table, y_back = jnp.asarray(table, BF), jnp.asarray(table.T, BF)
    tables = (y_table, y_back, x_tables[0], x_tables[1], *z_tables(), multiplier())
    (field_cb,) = call_transform(first_kernel, "pair_cb", tables, [*c, *b], [4])
    field_ca, c_keep, c_give = call_transform(
        second_kernel, "pair_ca", tables, [*c, *b, *a, field_cb], [4, 2, 2]
    )
    sums = add_halves(c_keep, to_mate(c_give))
    c_same, c_cross, field_ca = lax.optimization_barrier((*sums, field_ca))
    c_same, c_cross = send(c_same, 0, -2), send(c_cross, 2, -2)
    b_own, b_far, b_give, a_own, a_far, a_give = call_transform(
        third_kernel, "pair_ba", tables, [*c, *b, *a, field_cb, field_ca], [1, 1, 2, 1, 1, 2]
    )
    a_mate, b_mate = to_mate(a_give), to_mate(b_give)
    a_same = send(jnp.stack([a_own, a_mate[0]]), 0, 1)
    a_cross = send(jnp.stack([a_far, a_mate[1]]), 2, 1)
    b_cross = send(jnp.stack([b_far, b_mate[1]]), 2, 0)
    return unpack(place, a_same, a_cross, b_cross, b_own, b_mate, c_same, c_cross)


def solution(mesh):
    spec = P("band", "grid", None, None)
    return jax.shard_map(
        per_device, mesh=mesh, in_specs=(spec,), out_specs=spec, check_vma=False
    )
```

```python
import functools

import jax
import jax.numpy as jnp
import numpy as np
from jax import lax
from jax.experimental import pallas as pl
from jax.experimental.pallas import tpu as pltpu
from jax.sharding import PartitionSpec as P


NG = 96
PAIRS = 12
ROWS = 144
THIRD = 48
LANES = 128
SLAB = PAIRS * ROWS
KERNEL_SCALE = 16.0
SCREEN_SQ = 0.05
AXES = ("band", "grid")
BF = jnp.bfloat16
F32 = jnp.float32
BATCH = 6
STEPS = 4
SMALL_VMEM = 24 << 20
WHOLE_VMEM = 58 << 20
LARGE_VMEM = 30 << 20


def dft_table(length):
    half = length // 2
    rows = np.arange(length)
    freq = np.where(rows <= half, rows, rows - half)
    phase = 2.0 * np.pi * np.outer(freq, rows) / length
    return np.where((rows <= half)[:, None], np.cos(phase), np.sin(phase))


def z_tables():
    table = dft_table(NG)
    forward = np.zeros((3, LANES, 2 * LANES))
    inverse = np.zeros((3, 2 * LANES, LANES))
    for g in range(3):
        part = table[:, 32 * g : 32 * g + 32]
        forward[g, :NG, :NG] = table.T
        forward[g, NG:, LANES : LANES + NG] = part.T
        inverse[g, :NG, :NG] = table
        inverse[g, LANES : LANES + NG, NG:] = part
    return jnp.asarray(forward, BF), jnp.asarray(inverse, BF)


def frequency_weights(rows):
    freq = jnp.where(rows <= NG // 2, rows, rows - NG // 2).astype(F32)
    weight = jnp.where((rows == 0) | (rows == NG // 2), 1.0, 2.0) / NG
    return freq * freq, jnp.where(rows < NG, weight, 0.0)


def multiplier_kernel(out):
    dims = (NG, 2 * LANES)
    lane = lax.broadcasted_iota(jnp.int32, dims, 1)
    square_a, weight_a = frequency_weights(lax.broadcasted_iota(jnp.int32, dims, 0))
    square_c, weight_c = frequency_weights(lane % LANES)
    square = square_a + square_c + SCREEN_SQ
    scale = KERNEL_SCALE * weight_a * weight_c
    for q in range(NG // 2):
        even, odd = (frequency_weights(jnp.int32(2 * q + n)) for n in range(2))
        square_b, weight_b = (jnp.where(lane < LANES, *pair) for pair in zip(even, odd))
        out[q * NG : q * NG + NG, :] = scale * weight_b / (square + square_b)


def multiplier():
    return pl.pallas_call(
        multiplier_kernel,
        out_shape=jax.ShapeDtypeStruct((NG // 2 * NG, 2 * LANES), F32),
        compiler_params=pltpu.CompilerParams(vmem_limit_bytes=SMALL_VMEM),
        name="multiplier",
    )()


def dot(left, right):
    return jnp.dot(left, right, preferred_element_type=F32)


def pack_kernel(place, bands, for_a, for_b, b_keep, b_give, c_same, c_other):
    high, core = place[0], place[1]
    mix = high ^ core
    for p in range(bands.shape[1] // 2):
        packed = []
        for band in range(2):
            first, second = bands[band, 2 * p], bands[band, 2 * p + 1]
            heads = (first[:THIRD], first[THIRD:], second[:THIRD])
            rows = [
                jnp.concatenate([heads[g], second[THIRD:, 32 * g : 32 * g + 32]], axis=1)
                for g in range(3)
            ]
            packed.append(jnp.concatenate(rows, axis=0).astype(BF))
            for_a[core ^ band, p] = packed[band]
            for_b[1 - (mix ^ band), p] = packed[band]
        pick = lambda flag: jnp.where(flag == 0, packed[0], packed[1])
        b_keep[p], b_give[p] = pick(mix), pick(1 - mix)
        c_same[p], c_other[p] = pick(high), pick(1 - high)


def one_slab(per):
    return pl.BlockSpec((per, ROWS, LANES), lambda i: (i, 0, 0))


def two_slabs(per):
    return pl.BlockSpec((2, per, ROWS, LANES), lambda i: (0, i, 0, 0))


def shape_of(count):
    dims = (PAIRS, ROWS, LANES)
    return jax.ShapeDtypeStruct(dims if count == 1 else (count, *dims), BF)


def pack(place, bands):
    per = PAIRS // STEPS
    return pl.pallas_call(
        pack_kernel,
        grid=(STEPS,),
        in_specs=[
            pl.BlockSpec(memory_space=pltpu.SMEM),
            pl.BlockSpec((2, 2 * per, NG, NG), lambda i: (0, i, 0, 0)),
        ],
        out_specs=[two_slabs(per)] * 2 + [one_slab(per)] * 4,
        out_shape=[shape_of(2)] * 2 + [shape_of(1)] * 4,
        compiler_params=pltpu.CompilerParams(vmem_limit_bytes=WHOLE_VMEM),
        name="pack",
    )(place, bands)


def unpack_kernel(place, a_same, a_cross, b_cross, b_own, b_mate, c_same, c_cross, out):
    high, core = place[0], place[1]
    mix = high ^ core
    per = out.shape[1] // 2
    start = pl.program_id(0) * per
    for p in range(per):
        load = lambda ref, *at: ref[(*at, start + p)]
        for band in range(2):
            other = core ^ band
            third = jnp.where(mix == band, load(b_own), load(b_mate, 0)).astype(F32)
            fifth = jnp.where(high == band, load(c_same), load(c_cross)).astype(F32)
            total = load(a_same, other).astype(F32) + load(a_cross, other).astype(F32)
            total += third + load(b_cross, 1 - (mix ^ band)).astype(F32)
            total = -(total + fifth)
            out[band, 2 * p] = total[: 2 * THIRD, :NG]
            tail = [total[THIRD * g : THIRD * g + THIRD, NG:] for g in range(3)]
            out[band, 2 * p + 1, :THIRD] = total[2 * THIRD :, :NG]
            out[band, 2 * p + 1, THIRD:] = jnp.concatenate(tail, axis=1)


def unpack(place, *parts):
    per = PAIRS // STEPS
    return pl.pallas_call(
        unpack_kernel,
        grid=(STEPS,),
        in_specs=[pl.BlockSpec(memory_space=pltpu.SMEM)]
        + [pl.BlockSpec(memory_space=pltpu.VMEM)] * len(parts),
        out_specs=pl.BlockSpec((2, 2 * per, NG, NG), lambda i: (0, i, 0, 0)),
        out_shape=jax.ShapeDtypeStruct((2, 2 * PAIRS, NG, NG), F32),
        compiler_params=pltpu.CompilerParams(vmem_limit_bytes=SMALL_VMEM),
        name="unpack",
    )(place, *parts)


def transform(left, right, tables, grid_values, lines, emit):
    y_table, y_back, x_table, x_back, z_table, z_back, weights = tables
    flat = lambda v: v.reshape(-1, v.shape[-1])

    for r in range(4):
        held = lines.at[r % 2]

        def forward_z(i, carry, r=r, held=held):
            part = pl.ds(i * BATCH, BATCH)
            density = left[r][part] * right[r][part]
            sums = [
                dot(flat(density[:, THIRD * g : THIRD * g + THIRD]), z_table[g]) for g in range(3)
            ]
            tail = sums[0][:, LANES:] + sums[1][:, LANES:] + sums[2][:, LANES:]
            keep = lambda v: v.astype(BF).reshape(BATCH, THIRD, LANES)
            held[part, :THIRD, :LANES] = keep(sums[0][:, :LANES])
            held[part, THIRD:, :LANES] = keep(sums[1][:, :LANES])
            held[part, :THIRD, LANES:] = keep(sums[2][:, :LANES])
            held[part, THIRD:, LANES:] = keep(tail)
            return carry

        def forward_y(p, carry, r=r, held=held):
            values = dot(y_table[...], held[p])
            x = r * 2 * PAIRS + 2 * p
            grid_values[pl.ds(x, NG, stride=NG), :] = values[:, :LANES]
            grid_values[pl.ds(x + 1, NG, stride=NG), :] = values[:, LANES:]
            return carry

        lax.fori_loop(0, PAIRS // BATCH, forward_z, 0, unroll=True)
        lax.fori_loop(0, PAIRS, forward_y, 0, unroll=True)

    def middle(q, carry):
        upper = pl.ds(pl.multiple_of(q * 2 * NG, 2 * NG), NG)
        lower = pl.ds(pl.multiple_of(q * 2 * NG + NG, NG), NG)
        block = jnp.concatenate([grid_values[upper, :], grid_values[lower, :]], axis=1).astype(BF)
        scaled = weights[pl.ds(pl.multiple_of(q * NG, NG), NG), :] * dot(x_table[...], block)
        back = dot(x_back[...], scaled.astype(BF))
        grid_values[upper, :] = back[:, :LANES]
        grid_values[lower, :] = back[:, LANES:]
        return carry

    lax.fori_loop(0, NG // 2, middle, 0, unroll=True)

    for r in range(4):
        held = lines.at[r % 2]

        def inverse_y(p, carry, r=r, held=held):
            x = r * 2 * PAIRS + 2 * p
            one = grid_values[pl.ds(x, NG, stride=NG), :]
            two = grid_values[pl.ds(x + 1, NG, stride=NG), :]
            held[p] = dot(y_back[...], jnp.concatenate([one, two], axis=1).astype(BF)).astype(BF)
            return carry

        def inverse_z(i, carry, r=r, held=held):
            part = pl.ds(i * BATCH, BATCH)
            last = flat(held[part, THIRD:, LANES:])
            heads = (
                held[part, :THIRD, :LANES],
                held[part, THIRD:, :LANES],
                held[part, :THIRD, LANES:],
            )
            for g in range(3):
                values = dot(jnp.concatenate([flat(heads[g]), last], axis=1), z_back[g])
                at = (part, slice(THIRD * g, THIRD * g + THIRD))
                emit(r, at, values.astype(BF).reshape(BATCH, THIRD, LANES))
            return carry

        lax.fori_loop(0, PAIRS, inverse_y, 0, unroll=True)
        lax.fori_loop(0, PAIRS // BATCH, inverse_z, 0, unroll=True)


def slabs_of(refs, count):
    parts = [ref if len(ref.shape) == 3 else ref.at[0] for ref in refs[: 4 * count]]
    return [parts[4 * n : 4 * n + 4] for n in range(count)]


def first_kernel(*refs):
    c, b = slabs_of(refs[7:], 2)
    field_cb = refs[15]

    def emit(r, at, potential):
        field_cb[(r, *at)] = potential

    transform(c, b, refs[:7], *refs[16:], emit)


def second_kernel(*refs):
    c, b, a = slabs_of(refs[7:], 3)
    field_cb, field_ca, c_keep, c_give = refs[19:23]
    out = (c_keep.at[0], c_give.at[0], c_keep.at[1], c_give.at[1])

    def emit(r, at, potential):
        field_ca[(r, *at)] = potential
        total = field_cb[(r, *at)].astype(F32) * b[r][at].astype(F32)
        out[r][at] = (total + potential.astype(F32) * a[r][at].astype(F32)).astype(BF)

    transform(c, a, refs[:7], *refs[23:], emit)


def third_kernel(*refs):
    c, b, a = slabs_of(refs[7:], 3)
    field_cb, field_ca, b_own, b_far, b_give, a_own, a_far, a_give = refs[19:27]
    out_b = (b_own, b_give.at[0], b_far, b_give.at[1])
    out_a = (a_own, a_give.at[0], a_far, a_give.at[1])

    def emit(r, at, potential):
        field = potential.astype(F32)
        one, two, three = (v[r][at].astype(F32) for v in (c, b, a))
        out_b[r][at] = (field_cb[(r, *at)].astype(F32) * one + field * three).astype(BF)
        out_a[r][at] = (field_ca[(r, *at)].astype(F32) * one + field * two).astype(BF)

    transform(b, a, refs[:7], *refs[27:], emit)


def call_transform(kernel, name, tables, slabs, outs):
    return pl.pallas_call(
        kernel,
        in_specs=[pl.BlockSpec(memory_space=pltpu.VMEM)] * (len(tables) + len(slabs)),
        out_specs=[pl.BlockSpec(memory_space=pltpu.VMEM)] * len(outs),
        out_shape=[shape_of(count) for count in outs],
        scratch_shapes=[
            pltpu.VMEM((NG * NG, LANES), F32),
            pltpu.VMEM((2, PAIRS, NG, 2 * LANES), BF),
        ],
        compiler_params=pltpu.CompilerParams(vmem_limit_bytes=LARGE_VMEM),
        cost_estimate=pl.CostEstimate(
            flops=1 << 20, bytes_accessed=1 << 16, transcendentals=0
        ),
        name=name,
    )(*tables, *slabs)


def sum_kernel(kept, received, same, cross):
    for n, out in enumerate((same, cross)):
        out[...] = (kept[n].astype(F32) + received[n].astype(F32)).astype(BF)


def add_halves(kept, received):
    return pl.pallas_call(
        sum_kernel,
        out_shape=[shape_of(1)] * 2,
        compiler_params=pltpu.CompilerParams(vmem_limit_bytes=SMALL_VMEM),
        name="add_halves",
    )(kept, received)


def passed(value, blocks, by, length):
    pairs = [
        (4 * k + s, 4 * ((k + by) % length) + (s ^ blocks)) for k in range(length) for s in range(4)
    ]
    return lax.ppermute(value, AXES, pairs)


def per_device(bands):
    length = lax.axis_size("band")
    me = lax.axis_index("grid")
    place = jnp.stack([me // 2, me % 2]).astype(jnp.int32)
    send = functools.partial(passed, length=length)

    table = dft_table(NG)
    orders = [np.concatenate([np.arange(24) + 24 * (r ^ s) for r in range(4)]) for s in range(4)]
    both = np.stack([np.stack([table[:, order], table[:, order].T]) for order in orders])
    x_tables = lax.dynamic_index_in_dim(jnp.asarray(both, BF), me, 0, keepdims=False)

    for_a, for_b, b_keep, b_give, c_same, c_other = pack(place, bands)
    moved = (
        send(c_same, 0, 2),
        send(c_other, 2, 2),
        send(for_b, 2, 0),
        send(for_a, 0, -1),
        send(for_a, 2, -1),
    )
    moved, x_tables = lax.optimization_barrier((moved, x_tables))
    c_same, c_cross, b_cross, a_same, a_cross = moved
    to_mate = lambda value: send(value, 1, 0)
    b = [b_keep, to_mate(b_give), b_cross, to_mate(b_cross[1])]
    a = [a_same, to_mate(a_same[1]), a_cross, to_mate(a_cross[1])]

    c = [c_same, to_mate(c_same), c_cross, to_mate(c_cross)]

    y_table, y_back = jnp.asarray(table, BF), jnp.asarray(table.T, BF)
    tables = (y_table, y_back, x_tables[0], x_tables[1], *z_tables(), multiplier())
    (field_cb,) = call_transform(first_kernel, "pair_cb", tables, [*c, *b], [4])
    field_ca, c_keep, c_give = call_transform(
        second_kernel, "pair_ca", tables, [*c, *b, *a, field_cb], [4, 2, 2]
    )
    sums = add_halves(c_keep, to_mate(c_give))
    c_same, c_cross, field_ca = lax.optimization_barrier((*sums, field_ca))
    c_same, c_cross = send(c_same, 0, -2), send(c_cross, 2, -2)
    b_own, b_far, b_give, a_own, a_far, a_give = call_transform(
        third_kernel, "pair_ba", tables, [*c, *b, *a, field_cb, field_ca], [1, 1, 2, 1, 1, 2]
    )
    a_mate, b_mate = to_mate(a_give), to_mate(b_give)
    a_same = send(jnp.stack([a_own, a_mate[0]]), 0, 1)
    a_cross = send(jnp.stack([a_far, a_mate[1]]), 2, 1)
    b_cross = send(jnp.stack([b_far, b_mate[1]]), 2, 0)
    return unpack(place, a_same, a_cross, b_cross, b_own, b_mate, c_same, c_cross)


def solution(mesh):
    spec = P("band", "grid", None, None)
    return jax.shard_map(
        per_device, mesh=mesh, in_specs=(spec,), out_specs=spec, check_vma=False
    )
```

```python
import functools

import jax
import jax.numpy as jnp
import numpy as np
from jax import lax
from jax.experimental import pallas as pl
from jax.experimental.pallas import tpu as pltpu
from jax.sharding import PartitionSpec as P


NG = 96
PAIRS = 12
ROWS = 144
THIRD = 48
LANES = 128
SLAB = PAIRS * ROWS
KERNEL_SCALE = 16.0
SCREEN_SQ = 0.05
AXES = ("band", "grid")
BF = jnp.bfloat16
F32 = jnp.float32
BATCH = 6
STEPS = 2
SMALL_VMEM = 24 << 20
WHOLE_VMEM = 58 << 20
LARGE_VMEM = 30 << 20


def dft_table(length):
    half = length // 2
    rows = np.arange(length)
    freq = np.where(rows <= half, rows, rows - half)
    phase = 2.0 * np.pi * np.outer(freq, rows) / length
    return np.where((rows <= half)[:, None], np.cos(phase), np.sin(phase))


def z_tables():
    table = dft_table(NG)
    forward = np.zeros((3, LANES, 2 * LANES))
    inverse = np.zeros((3, 2 * LANES, LANES))
    for g in range(3):
        part = table[:, 32 * g : 32 * g + 32]
        forward[g, :NG, :NG] = table.T
        forward[g, NG:, LANES : LANES + NG] = part.T
        inverse[g, :NG, :NG] = table
        inverse[g, LANES : LANES + NG, NG:] = part
    return jnp.asarray(forward, BF), jnp.asarray(inverse, BF)


def frequency_weights(rows):
    freq = jnp.where(rows <= NG // 2, rows, rows - NG // 2).astype(F32)
    weight = jnp.where((rows == 0) | (rows == NG // 2), 1.0, 2.0) / NG
    return freq * freq, jnp.where(rows < NG, weight, 0.0)


def multiplier_kernel(out):
    dims = (NG, 2 * LANES)
    lane = lax.broadcasted_iota(jnp.int32, dims, 1)
    square_a, weight_a = frequency_weights(lax.broadcasted_iota(jnp.int32, dims, 0))
    square_c, weight_c = frequency_weights(lane % LANES)
    square = square_a + square_c + SCREEN_SQ
    scale = KERNEL_SCALE * weight_a * weight_c
    for q in range(NG // 2):
        even, odd = (frequency_weights(jnp.int32(2 * q + n)) for n in range(2))
        square_b, weight_b = (jnp.where(lane < LANES, *pair) for pair in zip(even, odd))
        out[q * NG : q * NG + NG, :] = scale * weight_b / (square + square_b)


def multiplier():
    return pl.pallas_call(
        multiplier_kernel,
        out_shape=jax.ShapeDtypeStruct((NG // 2 * NG, 2 * LANES), F32),
        compiler_params=pltpu.CompilerParams(vmem_limit_bytes=SMALL_VMEM),
        name="multiplier",
    )()


def dot(left, right):
    return jnp.dot(left, right, preferred_element_type=F32)


def pack_kernel(place, bands, for_a, for_b, b_keep, b_give, c_same, c_other):
    high, core = place[0], place[1]
    mix = high ^ core
    for p in range(bands.shape[1] // 2):
        packed = []
        for band in range(2):
            first, second = bands[band, 2 * p], bands[band, 2 * p + 1]
            heads = (first[:THIRD], first[THIRD:], second[:THIRD])
            rows = [
                jnp.concatenate([heads[g], second[THIRD:, 32 * g : 32 * g + 32]], axis=1)
                for g in range(3)
            ]
            packed.append(jnp.concatenate(rows, axis=0).astype(BF))
            for_a[core ^ band, p] = packed[band]
            for_b[1 - (mix ^ band), p] = packed[band]
        pick = lambda flag: jnp.where(flag == 0, packed[0], packed[1])
        b_keep[p], b_give[p] = pick(mix), pick(1 - mix)
        c_same[p], c_other[p] = pick(high), pick(1 - high)


def one_slab(per):
    return pl.BlockSpec((per, ROWS, LANES), lambda i: (i, 0, 0))


def two_slabs(per):
    return pl.BlockSpec((2, per, ROWS, LANES), lambda i: (0, i, 0, 0))


def shape_of(count):
    dims = (PAIRS, ROWS, LANES)
    return jax.ShapeDtypeStruct(dims if count == 1 else (count, *dims), BF)


def pack(place, bands):
    per = PAIRS // STEPS
    return pl.pallas_call(
        pack_kernel,
        grid=(STEPS,),
        in_specs=[
            pl.BlockSpec(memory_space=pltpu.SMEM),
            pl.BlockSpec((2, 2 * per, NG, NG), lambda i: (0, i, 0, 0)),
        ],
        out_specs=[two_slabs(per)] * 2 + [one_slab(per)] * 4,
        out_shape=[shape_of(2)] * 2 + [shape_of(1)] * 4,
        compiler_params=pltpu.CompilerParams(vmem_limit_bytes=WHOLE_VMEM),
        name="pack",
    )(place, bands)


def unpack_kernel(place, a_same, a_cross, b_cross, b_own, b_mate, c_same, c_cross, out):
    high, core = place[0], place[1]
    mix = high ^ core
    per = out.shape[1] // 2
    start = pl.program_id(0) * per
    for p in range(per):
        load = lambda ref, *at: ref[(*at, start + p)]
        for band in range(2):
            other = core ^ band
            third = jnp.where(mix == band, load(b_own), load(b_mate, 0)).astype(F32)
            fifth = jnp.where(high == band, load(c_same), load(c_cross)).astype(F32)
            total = load(a_same, other).astype(F32) + load(a_cross, other).astype(F32)
            total += third + load(b_cross, 1 - (mix ^ band)).astype(F32)
            total = -(total + fifth)
            out[band, 2 * p] = total[: 2 * THIRD, :NG]
            tail = [total[THIRD * g : THIRD * g + THIRD, NG:] for g in range(3)]
            out[band, 2 * p + 1, :THIRD] = total[2 * THIRD :, :NG]
            out[band, 2 * p + 1, THIRD:] = jnp.concatenate(tail, axis=1)


def unpack(place, *parts):
    per = PAIRS // STEPS
    return pl.pallas_call(
        unpack_kernel,
        grid=(STEPS,),
        in_specs=[pl.BlockSpec(memory_space=pltpu.SMEM)]
        + [pl.BlockSpec(memory_space=pltpu.VMEM)] * len(parts),
        out_specs=pl.BlockSpec((2, 2 * per, NG, NG), lambda i: (0, i, 0, 0)),
        out_shape=jax.ShapeDtypeStruct((2, 2 * PAIRS, NG, NG), F32),
        compiler_params=pltpu.CompilerParams(vmem_limit_bytes=SMALL_VMEM),
        name="unpack",
    )(place, *parts)


def transform(left, right, tables, grid_values, lines, emit):
    y_table, y_back, x_table, x_back, z_table, z_back, weights = tables
    flat = lambda v: v.reshape(-1, v.shape[-1])

    for r in range(4):
        held = lines.at[r % 2]

        def forward_z(i, carry, r=r, held=held):
            part = pl.ds(i * BATCH, BATCH)
            density = left[r][part] * right[r][part]
            sums = [
                dot(flat(density[:, THIRD * g : THIRD * g + THIRD]), z_table[g]) for g in range(3)
            ]
            tail = sums[0][:, LANES:] + sums[1][:, LANES:] + sums[2][:, LANES:]
            keep = lambda v: v.astype(BF).reshape(BATCH, THIRD, LANES)
            held[part, :THIRD, :LANES] = keep(sums[0][:, :LANES])
            held[part, THIRD:, :LANES] = keep(sums[1][:, :LANES])
            held[part, :THIRD, LANES:] = keep(sums[2][:, :LANES])
            held[part, THIRD:, LANES:] = keep(tail)
            return carry

        def forward_y(p, carry, r=r, held=held):
            values = dot(y_table[...], held[p])
            x = r * 2 * PAIRS + 2 * p
            grid_values[pl.ds(x, NG, stride=NG), :] = values[:, :LANES]
            grid_values[pl.ds(x + 1, NG, stride=NG), :] = values[:, LANES:]
            return carry

        lax.fori_loop(0, PAIRS // BATCH, forward_z, 0, unroll=True)
        lax.fori_loop(0, PAIRS, forward_y, 0, unroll=True)

    def middle(q, carry):
        upper = pl.ds(pl.multiple_of(q * 2 * NG, 2 * NG), NG)
        lower = pl.ds(pl.multiple_of(q * 2 * NG + NG, NG), NG)
        block = jnp.concatenate([grid_values[upper, :], grid_values[lower, :]], axis=1).astype(BF)
        scaled = weights[pl.ds(pl.multiple_of(q * NG, NG), NG), :] * dot(x_table[...], block)
        back = dot(x_back[...], scaled.astype(BF))
        grid_values[upper, :] = back[:, :LANES]
        grid_values[lower, :] = back[:, LANES:]
        return carry

    lax.fori_loop(0, NG // 2, middle, 0, unroll=True)

    for r in range(4):
        held = lines.at[r % 2]

        def inverse_y(p, carry, r=r, held=held):
            x = r * 2 * PAIRS + 2 * p
            one = grid_values[pl.ds(x, NG, stride=NG), :]
            two = grid_values[pl.ds(x + 1, NG, stride=NG), :]
            held[p] = dot(y_back[...], jnp.concatenate([one, two], axis=1).astype(BF)).astype(BF)
            return carry

        def inverse_z(i, carry, r=r, held=held):
            part = pl.ds(i * BATCH, BATCH)
            last = flat(held[part, THIRD:, LANES:])
            heads = (
                held[part, :THIRD, :LANES],
                held[part, THIRD:, :LANES],
                held[part, :THIRD, LANES:],
            )
            for g in range(3):
                values = dot(jnp.concatenate([flat(heads[g]), last], axis=1), z_back[g])
                at = (part, slice(THIRD * g, THIRD * g + THIRD))
                emit(r, at, values.astype(BF).reshape(BATCH, THIRD, LANES))
            return carry

        lax.fori_loop(0, PAIRS, inverse_y, 0, unroll=True)
        lax.fori_loop(0, PAIRS // BATCH, inverse_z, 0, unroll=True)


def slabs_of(refs, count):
    parts = [ref if len(ref.shape) == 3 else ref.at[0] for ref in refs[: 4 * count]]
    return [parts[4 * n : 4 * n + 4] for n in range(count)]


def first_kernel(*refs):
    c, b = slabs_of(refs[7:], 2)
    field_cb = refs[15]

    def emit(r, at, potential):
        field_cb[(r, *at)] = potential

    transform(c, b, refs[:7], *refs[16:], emit)


def second_kernel(*refs):
    c, b, a = slabs_of(refs[7:], 3)
    field_cb, field_ca, c_keep, c_give = refs[19:23]
    out = (c_keep.at[0], c_give.at[0], c_keep.at[1], c_give.at[1])

    def emit(r, at, potential):
        field_ca[(r, *at)] = potential
        total = field_cb[(r, *at)].astype(F32) * b[r][at].astype(F32)
        out[r][at] = (total + potential.astype(F32) * a[r][at].astype(F32)).astype(BF)

    transform(c, a, refs[:7], *refs[23:], emit)


def third_kernel(*refs):
    c, b, a = slabs_of(refs[7:], 3)
    field_cb, field_ca, b_own, b_far, b_give, a_own, a_far, a_give = refs[19:27]
    out_b = (b_own, b_give.at[0], b_far, b_give.at[1])
    out_a = (a_own, a_give.at[0], a_far, a_give.at[1])

    def emit(r, at, potential):
        field = potential.astype(F32)
        one, two, three = (v[r][at].astype(F32) for v in (c, b, a))
        out_b[r][at] = (field_cb[(r, *at)].astype(F32) * one + field * three).astype(BF)
        out_a[r][at] = (field_ca[(r, *at)].astype(F32) * one + field * two).astype(BF)

    transform(b, a, refs[:7], *refs[27:], emit)


def call_transform(kernel, name, tables, slabs, outs):
    return pl.pallas_call(
        kernel,
        in_specs=[pl.BlockSpec(memory_space=pltpu.VMEM)] * (len(tables) + len(slabs)),
        out_specs=[pl.BlockSpec(memory_space=pltpu.VMEM)] * len(outs),
        out_shape=[shape_of(count) for count in outs],
        scratch_shapes=[
            pltpu.VMEM((NG * NG, LANES), F32),
            pltpu.VMEM((2, PAIRS, NG, 2 * LANES), BF),
        ],
        compiler_params=pltpu.CompilerParams(vmem_limit_bytes=LARGE_VMEM),
        cost_estimate=pl.CostEstimate(
            flops=1 << 20, bytes_accessed=1 << 16, transcendentals=0
        ),
        name=name,
    )(*tables, *slabs)


def sum_kernel(kept, received, same, cross):
    for n, out in enumerate((same, cross)):
        out[...] = (kept[n].astype(F32) + received[n].astype(F32)).astype(BF)


def add_halves(kept, received):
    return pl.pallas_call(
        sum_kernel,
        out_shape=[shape_of(1)] * 2,
        compiler_params=pltpu.CompilerParams(vmem_limit_bytes=SMALL_VMEM),
        name="add_halves",
    )(kept, received)


def passed(value, blocks, by, length):
    pairs = [
        (4 * k + s, 4 * ((k + by) % length) + (s ^ blocks)) for k in range(length) for s in range(4)
    ]
    return lax.ppermute(value, AXES, pairs)


def per_device(bands):
    length = lax.axis_size("band")
    me = lax.axis_index("grid")
    place = jnp.stack([me // 2, me % 2]).astype(jnp.int32)
    send = functools.partial(passed, length=length)

    table = dft_table(NG)
    orders = [np.concatenate([np.arange(24) + 24 * (r ^ s) for r in range(4)]) for s in range(4)]
    both = np.stack([np.stack([table[:, order], table[:, order].T]) for order in orders])
    x_tables = lax.dynamic_index_in_dim(jnp.asarray(both, BF), me, 0, keepdims=False)

    for_a, for_b, b_keep, b_give, c_same, c_other = pack(place, bands)
    moved = (
        send(c_same, 0, 2),
        send(c_other, 2, 2),
        send(for_b, 2, 0),
        send(for_a, 0, -1),
        send(for_a, 2, -1),
    )
    moved, x_tables = lax.optimization_barrier((moved, x_tables))
    c_same, c_cross, b_cross, a_same, a_cross = moved
    to_mate = lambda value: send(value, 1, 0)
    b = [b_keep, to_mate(b_give), b_cross, to_mate(b_cross[1])]
    a = [a_same, to_mate(a_same[1]), a_cross, to_mate(a_cross[1])]

    c = [c_same, to_mate(c_same), c_cross, to_mate(c_cross)]

    y_table, y_back = jnp.asarray(table, BF), jnp.asarray(table.T, BF)
    tables = (y_table, y_back, x_tables[0], x_tables[1], *z_tables(), multiplier())
    (field_cb,) = call_transform(first_kernel, "pair_cb", tables, [*c, *b], [4])
    field_ca, c_keep, c_give = call_transform(
        second_kernel, "pair_ca", tables, [*c, *b, *a, field_cb], [4, 2, 2]
    )
    sums = add_halves(c_keep, to_mate(c_give))
    c_same, c_cross, field_ca = lax.optimization_barrier((*sums, field_ca))
    c_same, c_cross = send(c_same, 0, -2), send(c_cross, 2, -2)
    b_own, b_far, b_give, a_own, a_far, a_give = call_transform(
        third_kernel, "pair_ba", tables, [*c, *b, *a, field_cb, field_ca], [1, 1, 2, 1, 1, 2]
    )
    a_mate, b_mate = to_mate(a_give), to_mate(b_give)
    a_same = send(jnp.stack([a_own, a_mate[0]]), 0, 1)
    a_cross = send(jnp.stack([a_far, a_mate[1]]), 2, 1)
    b_cross = send(jnp.stack([b_far, b_mate[1]]), 2, 0)
    return unpack(place, a_same, a_cross, b_cross, b_own, b_mate, c_same, c_cross)


def solution(mesh):
    spec = P("band", "grid", None, None)
    return jax.shard_map(
        per_device, mesh=mesh, in_specs=(spec,), out_specs=spec, check_vma=False
    )
```

```python
import functools

import jax
import jax.numpy as jnp
import numpy as np
from jax import lax
from jax.experimental import pallas as pl
from jax.experimental.pallas import tpu as pltpu
from jax.sharding import PartitionSpec as P


NG = 96
PAIRS = 12
ROWS = 144
THIRD = 48
LANES = 128
SLAB = PAIRS * ROWS
KERNEL_SCALE = 16.0
SCREEN_SQ = 0.05
AXES = ("band", "grid")
BF = jnp.bfloat16
F32 = jnp.float32
BATCH = 12
STEPS = 2
SMALL_VMEM = 24 << 20
WHOLE_VMEM = 58 << 20
LARGE_VMEM = 30 << 20


def dft_table(length):
    half = length // 2
    rows = np.arange(length)
    freq = np.where(rows <= half, rows, rows - half)
    phase = 2.0 * np.pi * np.outer(freq, rows) / length
    return np.where((rows <= half)[:, None], np.cos(phase), np.sin(phase))


def z_tables():
    table = dft_table(NG)
    forward = np.zeros((3, LANES, 2 * LANES))
    inverse = np.zeros((3, 2 * LANES, LANES))
    for g in range(3):
        part = table[:, 32 * g : 32 * g + 32]
        forward[g, :NG, :NG] = table.T
        forward[g, NG:, LANES : LANES + NG] = part.T
        inverse[g, :NG, :NG] = table
        inverse[g, LANES : LANES + NG, NG:] = part
    return jnp.asarray(forward, BF), jnp.asarray(inverse, BF)


def frequency_weights(rows):
    freq = jnp.where(rows <= NG // 2, rows, rows - NG // 2).astype(F32)
    weight = jnp.where((rows == 0) | (rows == NG // 2), 1.0, 2.0) / NG
    return freq * freq, jnp.where(rows < NG, weight, 0.0)


def multiplier_kernel(out):
    dims = (NG, 2 * LANES)
    lane = lax.broadcasted_iota(jnp.int32, dims, 1)
    square_a, weight_a = frequency_weights(lax.broadcasted_iota(jnp.int32, dims, 0))
    square_c, weight_c = frequency_weights(lane % LANES)
    square = square_a + square_c + SCREEN_SQ
    scale = KERNEL_SCALE * weight_a * weight_c
    for q in range(NG // 2):
        even, odd = (frequency_weights(jnp.int32(2 * q + n)) for n in range(2))
        square_b, weight_b = (jnp.where(lane < LANES, *pair) for pair in zip(even, odd))
        out[q * NG : q * NG + NG, :] = scale * weight_b / (square + square_b)


def multiplier():
    return pl.pallas_call(
        multiplier_kernel,
        out_shape=jax.ShapeDtypeStruct((NG // 2 * NG, 2 * LANES), F32),
        compiler_params=pltpu.CompilerParams(vmem_limit_bytes=SMALL_VMEM),
        name="multiplier",
    )()


def dot(left, right):
    return jnp.dot(left, right, preferred_element_type=F32)


def pack_kernel(place, bands, for_a, for_b, b_keep, b_give, c_same, c_other):
    high, core = place[0], place[1]
    mix = high ^ core
    for p in range(bands.shape[1] // 2):
        packed = []
        for band in range(2):
            first, second = bands[band, 2 * p], bands[band, 2 * p + 1]
            heads = (first[:THIRD], first[THIRD:], second[:THIRD])
            rows = [
                jnp.concatenate([heads[g], second[THIRD:, 32 * g : 32 * g + 32]], axis=1)
                for g in range(3)
            ]
            packed.append(jnp.concatenate(rows, axis=0).astype(BF))
            for_a[core ^ band, p] = packed[band]
            for_b[1 - (mix ^ band), p] = packed[band]
        pick = lambda flag: jnp.where(flag == 0, packed[0], packed[1])
        b_keep[p], b_give[p] = pick(mix), pick(1 - mix)
        c_same[p], c_other[p] = pick(high), pick(1 - high)


def one_slab(per):
    return pl.BlockSpec((per, ROWS, LANES), lambda i: (i, 0, 0))


def two_slabs(per):
    return pl.BlockSpec((2, per, ROWS, LANES), lambda i: (0, i, 0, 0))


def shape_of(count):
    dims = (PAIRS, ROWS, LANES)
    return jax.ShapeDtypeStruct(dims if count == 1 else (count, *dims), BF)


def pack(place, bands):
    per = PAIRS // STEPS
    return pl.pallas_call(
        pack_kernel,
        grid=(STEPS,),
        in_specs=[
            pl.BlockSpec(memory_space=pltpu.SMEM),
            pl.BlockSpec((2, 2 * per, NG, NG), lambda i: (0, i, 0, 0)),
        ],
        out_specs=[two_slabs(per)] * 2 + [one_slab(per)] * 4,
        out_shape=[shape_of(2)] * 2 + [shape_of(1)] * 4,
        compiler_params=pltpu.CompilerParams(vmem_limit_bytes=WHOLE_VMEM),
        name="pack",
    )(place, bands)


def unpack_kernel(place, a_same, a_cross, b_cross, b_own, b_mate, c_same, c_cross, out):
    high, core = place[0], place[1]
    mix = high ^ core
    per = out.shape[1] // 2
    start = pl.program_id(0) * per
    for p in range(per):
        load = lambda ref, *at: ref[(*at, start + p)]
        for band in range(2):
            other = core ^ band
            third = jnp.where(mix == band, load(b_own), load(b_mate, 0)).astype(F32)
            fifth = jnp.where(high == band, load(c_same), load(c_cross)).astype(F32)
            total = load(a_same, other).astype(F32) + load(a_cross, other).astype(F32)
            total += third + load(b_cross, 1 - (mix ^ band)).astype(F32)
            total = -(total + fifth)
            out[band, 2 * p] = total[: 2 * THIRD, :NG]
            tail = [total[THIRD * g : THIRD * g + THIRD, NG:] for g in range(3)]
            out[band, 2 * p + 1, :THIRD] = total[2 * THIRD :, :NG]
            out[band, 2 * p + 1, THIRD:] = jnp.concatenate(tail, axis=1)


def unpack(place, *parts):
    per = PAIRS // STEPS
    return pl.pallas_call(
        unpack_kernel,
        grid=(STEPS,),
        in_specs=[pl.BlockSpec(memory_space=pltpu.SMEM)]
        + [pl.BlockSpec(memory_space=pltpu.VMEM)] * len(parts),
        out_specs=pl.BlockSpec((2, 2 * per, NG, NG), lambda i: (0, i, 0, 0)),
        out_shape=jax.ShapeDtypeStruct((2, 2 * PAIRS, NG, NG), F32),
        compiler_params=pltpu.CompilerParams(vmem_limit_bytes=SMALL_VMEM),
        name="unpack",
    )(place, *parts)


def transform(left, right, tables, grid_values, lines, emit):
    y_table, y_back, x_table, x_back, z_table, z_back, weights = tables
    flat = lambda v: v.reshape(-1, v.shape[-1])

    for r in range(4):
        held = lines.at[r % 2]

        def forward_z(i, carry, r=r, held=held):
            part = pl.ds(i * BATCH, BATCH)
            density = left[r][part] * right[r][part]
            sums = [
                dot(flat(density[:, THIRD * g : THIRD * g + THIRD]), z_table[g]) for g in range(3)
            ]
            tail = sums[0][:, LANES:] + sums[1][:, LANES:] + sums[2][:, LANES:]
            keep = lambda v: v.astype(BF).reshape(BATCH, THIRD, LANES)
            held[part, :THIRD, :LANES] = keep(sums[0][:, :LANES])
            held[part, THIRD:, :LANES] = keep(sums[1][:, :LANES])
            held[part, :THIRD, LANES:] = keep(sums[2][:, :LANES])
            held[part, THIRD:, LANES:] = keep(tail)
            return carry

        def forward_y(p, carry, r=r, held=held):
            values = dot(y_table[...], held[p])
            x = r * 2 * PAIRS + 2 * p
            grid_values[pl.ds(x, NG, stride=NG), :] = values[:, :LANES]
            grid_values[pl.ds(x + 1, NG, stride=NG), :] = values[:, LANES:]
            return carry

        lax.fori_loop(0, PAIRS // BATCH, forward_z, 0, unroll=True)
        lax.fori_loop(0, PAIRS, forward_y, 0, unroll=True)

    def middle(q, carry):
        upper = pl.ds(pl.multiple_of(q * 2 * NG, 2 * NG), NG)
        lower = pl.ds(pl.multiple_of(q * 2 * NG + NG, NG), NG)
        block = jnp.concatenate([grid_values[upper, :], grid_values[lower, :]], axis=1).astype(BF)
        scaled = weights[pl.ds(pl.multiple_of(q * NG, NG), NG), :] * dot(x_table[...], block)
        back = dot(x_back[...], scaled.astype(BF))
        grid_values[upper, :] = back[:, :LANES]
        grid_values[lower, :] = back[:, LANES:]
        return carry

    lax.fori_loop(0, NG // 2, middle, 0, unroll=True)

    for r in range(4):
        held = lines.at[r % 2]

        def inverse_y(p, carry, r=r, held=held):
            x = r * 2 * PAIRS + 2 * p
            one = grid_values[pl.ds(x, NG, stride=NG), :]
            two = grid_values[pl.ds(x + 1, NG, stride=NG), :]
            held[p] = dot(y_back[...], jnp.concatenate([one, two], axis=1).astype(BF)).astype(BF)
            return carry

        def inverse_z(i, carry, r=r, held=held):
            part = pl.ds(i * BATCH, BATCH)
            last = flat(held[part, THIRD:, LANES:])
            heads = (
                held[part, :THIRD, :LANES],
                held[part, THIRD:, :LANES],
                held[part, :THIRD, LANES:],
            )
            for g in range(3):
                values = dot(jnp.concatenate([flat(heads[g]), last], axis=1), z_back[g])
                at = (part, slice(THIRD * g, THIRD * g + THIRD))
                emit(r, at, values.astype(BF).reshape(BATCH, THIRD, LANES))
            return carry

        lax.fori_loop(0, PAIRS, inverse_y, 0, unroll=True)
        lax.fori_loop(0, PAIRS // BATCH, inverse_z, 0, unroll=True)


def slabs_of(refs, count):
    parts = [ref if len(ref.shape) == 3 else ref.at[0] for ref in refs[: 4 * count]]
    return [parts[4 * n : 4 * n + 4] for n in range(count)]


def first_kernel(*refs):
    c, b = slabs_of(refs[7:], 2)
    field_cb = refs[15]

    def emit(r, at, potential):
        field_cb[(r, *at)] = potential

    transform(c, b, refs[:7], *refs[16:], emit)


def second_kernel(*refs):
    c, b, a = slabs_of(refs[7:], 3)
    field_cb, field_ca, c_keep, c_give = refs[19:23]
    out = (c_keep.at[0], c_give.at[0], c_keep.at[1], c_give.at[1])

    def emit(r, at, potential):
        field_ca[(r, *at)] = potential
        total = field_cb[(r, *at)].astype(F32) * b[r][at].astype(F32)
        out[r][at] = (total + potential.astype(F32) * a[r][at].astype(F32)).astype(BF)

    transform(c, a, refs[:7], *refs[23:], emit)


def third_kernel(*refs):
    c, b, a = slabs_of(refs[7:], 3)
    field_cb, field_ca, b_own, b_far, b_give, a_own, a_far, a_give = refs[19:27]
    out_b = (b_own, b_give.at[0], b_far, b_give.at[1])
    out_a = (a_own, a_give.at[0], a_far, a_give.at[1])

    def emit(r, at, potential):
        field = potential.astype(F32)
        one, two, three = (v[r][at].astype(F32) for v in (c, b, a))
        out_b[r][at] = (field_cb[(r, *at)].astype(F32) * one + field * three).astype(BF)
        out_a[r][at] = (field_ca[(r, *at)].astype(F32) * one + field * two).astype(BF)

    transform(b, a, refs[:7], *refs[27:], emit)


def call_transform(kernel, name, tables, slabs, outs):
    return pl.pallas_call(
        kernel,
        in_specs=[pl.BlockSpec(memory_space=pltpu.VMEM)] * (len(tables) + len(slabs)),
        out_specs=[pl.BlockSpec(memory_space=pltpu.VMEM)] * len(outs),
        out_shape=[shape_of(count) for count in outs],
        scratch_shapes=[
            pltpu.VMEM((NG * NG, LANES), F32),
            pltpu.VMEM((2, PAIRS, NG, 2 * LANES), BF),
        ],
        compiler_params=pltpu.CompilerParams(vmem_limit_bytes=LARGE_VMEM),
        cost_estimate=pl.CostEstimate(
            flops=1 << 20, bytes_accessed=1 << 16, transcendentals=0
        ),
        name=name,
    )(*tables, *slabs)


def sum_kernel(kept, received, same, cross):
    for n, out in enumerate((same, cross)):
        out[...] = (kept[n].astype(F32) + received[n].astype(F32)).astype(BF)


def add_halves(kept, received):
    return pl.pallas_call(
        sum_kernel,
        out_shape=[shape_of(1)] * 2,
        compiler_params=pltpu.CompilerParams(vmem_limit_bytes=SMALL_VMEM),
        name="add_halves",
    )(kept, received)


def passed(value, blocks, by, length):
    pairs = [
        (4 * k + s, 4 * ((k + by) % length) + (s ^ blocks)) for k in range(length) for s in range(4)
    ]
    return lax.ppermute(value, AXES, pairs)


def per_device(bands):
    length = lax.axis_size("band")
    me = lax.axis_index("grid")
    place = jnp.stack([me // 2, me % 2]).astype(jnp.int32)
    send = functools.partial(passed, length=length)

    table = dft_table(NG)
    orders = [np.concatenate([np.arange(24) + 24 * (r ^ s) for r in range(4)]) for s in range(4)]
    both = np.stack([np.stack([table[:, order], table[:, order].T]) for order in orders])
    x_tables = lax.dynamic_index_in_dim(jnp.asarray(both, BF), me, 0, keepdims=False)

    for_a, for_b, b_keep, b_give, c_same, c_other = pack(place, bands)
    moved = (
        send(c_same, 0, 2),
        send(c_other, 2, 2),
        send(for_b, 2, 0),
        send(for_a, 0, -1),
        send(for_a, 2, -1),
    )
    moved, x_tables = lax.optimization_barrier((moved, x_tables))
    c_same, c_cross, b_cross, a_same, a_cross = moved
    to_mate = lambda value: send(value, 1, 0)
    b = [b_keep, to_mate(b_give), b_cross, to_mate(b_cross[1])]
    a = [a_same, to_mate(a_same[1]), a_cross, to_mate(a_cross[1])]

    c = [c_same, to_mate(c_same), c_cross, to_mate(c_cross)]

    y_table, y_back = jnp.asarray(table, BF), jnp.asarray(table.T, BF)
    tables = (y_table, y_back, x_tables[0], x_tables[1], *z_tables(), multiplier())
    (field_cb,) = call_transform(first_kernel, "pair_cb", tables, [*c, *b], [4])
    field_ca, c_keep, c_give = call_transform(
        second_kernel, "pair_ca", tables, [*c, *b, *a, field_cb], [4, 2, 2]
    )
    sums = add_halves(c_keep, to_mate(c_give))
    c_same, c_cross, field_ca = lax.optimization_barrier((*sums, field_ca))
    c_same, c_cross = send(c_same, 0, -2), send(c_cross, 2, -2)
    b_own, b_far, b_give, a_own, a_far, a_give = call_transform(
        third_kernel, "pair_ba", tables, [*c, *b, *a, field_cb, field_ca], [1, 1, 2, 1, 1, 2]
    )
    a_mate, b_mate = to_mate(a_give), to_mate(b_give)
    a_same = send(jnp.stack([a_own, a_mate[0]]), 0, 1)
    a_cross = send(jnp.stack([a_far, a_mate[1]]), 2, 1)
    b_cross = send(jnp.stack([b_far, b_mate[1]]), 2, 0)
    return unpack(place, a_same, a_cross, b_cross, b_own, b_mate, c_same, c_cross)


def solution(mesh):
    spec = P("band", "grid", None, None)
    return jax.shard_map(
        per_device, mesh=mesh, in_specs=(spec,), out_specs=spec, check_vma=False
    )
```
